512 devices in a mesh: group: 16 (over y, z_lo), brick: 32 (over x, z_hi, core).
Axes of the slice: x: 4, y: 8, z: 8 (z_hi: 4, z_lo: 2; z = z_hi * 2 + z_lo), core: 2. Of those that a mesh axis runs over, the one named last changes fastest.
Arguments:
- populations: float32 [19, 32, 128, 128], P(None, 'brick', 'group'), may hold values from 0.5 to 1.5
- membrane_rows: int32 [32, 128], P('brick'), may hold values from 60 to 67
- positions: float32 [16, 3, 16, 32, 128], P('group', None, None, 'brick'), may hold values from 0 to 1
- velocities: float32 [16, 3, 16, 32, 128], P('group', None, None, 'brick'), may hold values from -4 to 4
- kicks: float32 [16, 3, 16, 32, 128], P('group', None, None, 'brick'), may hold values from -5 to 5
- bead_types: int32 [16, 16, 32, 128], P('group', None, 'brick'), may hold values from 0 to 1
- bond_partner: int32 [16, 16, 32, 128], P('group', None, 'brick'), may hold values from 0 to 15, as said below
- tile_counts: int32 [16, 32, 128], P('group', 'brick'), may hold values from 4 to 16
Outputs:
- new_populations: float32 [19, 32, 128, 128], P(None, 'brick', 'group')
- cell_mean: float32 [3, 32, 128], P(None, 'brick')
- new_positions: float32 [16, 3, 16, 32, 128], P('group', None, None, 'brick')
- new_velocities: float32 [16, 3, 16, 32, 128], P('group', None, None, 'brick')
The draws below stay inside these ranges and needn't reach their ends.
Inputs may be any that keep to these rules, and one draw needn't show every extreme that they name: bond_partner pairs slots of one tile: the partner of a slot's partner is the slot itself; a slot that is its own partner has no bond.
All inputs are finite; a program needn't handle non-finite values.
Results may differ from the reference program's by a relative error of at most 0.0003.
Values sent between devices are 32-bit elements; how exact they have to be, the bound alone decides.
A program may use at most 64 MiB of HBM per device.

```python
import math
import jax
import jax.numpy as jnp
import numpy as np
from jax import lax

LY = 8
NZ = 128
CAP = 16
STEPS = 3
REPLICAS = 16
NX = 32
NY = 128


def draw_bond_partner(key, part):
    tile_count = REPLICAS * NX * NZ
    scores = jax.random.randint(jax.random.fold_in(key, 11), (tile_count, CAP), 0, 1 << 20) * CAP + jnp.arange(CAP, dtype=jnp.int32)[None]
    ranking = jnp.argsort(scores, axis=1, stable=True).astype(jnp.int32)
    partners = ranking[:, np.arange(CAP) ^ 1]
    single = jax.random.randint(jax.random.fold_in(key, 12), (tile_count, CAP // 2), 0, 4) == 0
    single_slots = jnp.repeat(single, 2, axis=1)
    partners = jnp.where(single_slots, ranking, partners)
    tile_rows = jnp.arange(tile_count, dtype=jnp.int32)[:, None]
    result = jnp.zeros((tile_count, CAP), jnp.int32).at[tile_rows, ranking].set(partners)
    return result.reshape(REPLICAS, NX, NZ, CAP).transpose(0, 3, 1, 2)


def touch_ends(values, rng, least, top_value):
    dims = values.shape
    spot = [jax.random.randint(jax.random.fold_in(rng, axis), (), 0, dims[axis]) for axis in range(len(dims))]
    values = values.at[tuple(spot)].set(least)
    longest = dims.index(max(dims))
    spot[longest] = (spot[longest] + 1) % dims[longest]
    return values.at[tuple(spot)].set(top_value)


def shard_levels(rng, shape, shards, smallest, largest):
    loudness, own = 1.0, jax.random.fold_in(rng, 6)
    for position, blocks in shards:
        heights = jnp.exp(jax.random.uniform(jax.random.fold_in(own, position), (blocks,), jnp.float32, smallest / len(shards), largest / len(shards)))
        loudness = loudness * jnp.repeat(heights, shape[position] // blocks).reshape([-1 if axis == position else 1 for axis in range(len(shape))])
    return loudness


def scatter_about(stream_key, extent, width, limit, shards=(), held_as=jnp.bfloat16):
    drawn = jax.random.normal(stream_key, extent, jnp.float32) * width
    if len(shards) > 0:
        drawn = shard_levels(stream_key, extent, shards, -0.22, 0.18) * drawn
    return jnp.clip(drawn, min=-limit, max=limit).astype(held_as)


def setup_inputs(seed: int = 0) -> dict:
    streams_of = jax.random.split(jax.random.key(seed), 9)
    populations = jnp.clip(0.5 + 1.0 * jax.random.uniform(streams_of[0], (19, NX, NY, NZ), jnp.float32) ** shard_levels(streams_of[0], (19, NX, NY, NZ), ((1, 32), (2, 16)), -0.2, 0.2), 0.5, 1.5)
    membrane_rows = touch_ends(jax.random.randint(streams_of[1], (NX, NZ), NY // 2 - LY // 2, NY // 2 + LY // 2), jax.random.fold_in(streams_of[1], 1), NY // 2 - LY // 2, (NY // 2 + LY // 2) - 1).astype(jnp.int32)
    positions = jnp.clip(1.0 * jax.random.uniform(streams_of[2], (REPLICAS, 3, CAP, NX, NZ), jnp.float32) ** shard_levels(streams_of[2], (REPLICAS, 3, CAP, NX, NZ), ((0, 16), (3, 32)), -0.2, 0.2), 0.0, 1.0)
    velocities = scatter_about(streams_of[3], (REPLICAS, 3, CAP, NX, NZ), 1.0, 4.0, ((0, 16), (3, 32)), jnp.float32)
    kicks = scatter_about(streams_of[4], (REPLICAS, STEPS, CAP, NX, NZ), 1.0, 5.0, ((0, 16), (3, 32)), jnp.float32)
    bead_types = touch_ends(jax.random.randint(streams_of[5], (REPLICAS, CAP, NX, NZ), 0, 2), jax.random.fold_in(streams_of[5], 1), 0, 1).astype(jnp.int32)
    bond_partner = draw_bond_partner(jax.random.fold_in(streams_of[8], 71), 0)
    tile_counts = touch_ends(jax.random.randint(streams_of[7], (REPLICAS, NX, NZ), CAP // 4, CAP + 1), jax.random.fold_in(streams_of[7], 1), CAP // 4, CAP).astype(jnp.int32)
    return dict(populations=populations, membrane_rows=membrane_rows, positions=positions, velocities=velocities, kicks=kicks, bead_types=bead_types, bond_partner=bond_partner, tile_counts=tile_counts)


VELOCITY_SET = np.array([[0, 0, 0], [1, 0, 0], [-1, 0, 0], [0, 1, 0], [0, -1, 0], [0, 0, 1], [0, 0, -1], [1, 1, 0], [-1, -1, 0], [1, -1, 0], [-1, 1, 0], [1, 0, 1], [-1, 0, -1], [1, 0, -1], [-1, 0, 1], [0, 1, 1], [0, -1, -1], [0, 1, -1], [0, -1, 1]], dtype=np.int32)
WEIGHT_SET = np.array([1.0 / 3.0] + [1.0 / 18.0] * 6 + [1.0 / 36.0] * 12)
OPPOSITE = (0, 2, 1, 4, 3, 6, 5, 8, 7, 10, 9, 12, 11, 14, 13, 16, 15, 18, 17)
FROM_BELOW = (3, 7, 10, 15, 17)
FROM_ABOVE = (4, 8, 9, 16, 18)
RELAX_TIME = 0.8
PUSH_VECTOR = (0.001, 0.0, 0.0)
COUPLE_RATE = 1.0
VELOCITY_SCALE = 0.1
DRAG_RATE = 5.0
REPEL_SAME = 25.0
REPEL_CROSS = 50.0
FRICTION = 4.5
NOISE_SCALE = 3.0 / math.sqrt(0.02)
TIME_STEP = 0.02
BOND_STIFF = 10.0
HALF_ROOT = 1.0 / math.sqrt(2.0)
HIGHEST = lax.Precision.HIGHEST

def moments(lattice):
    weights = jnp.asarray(WEIGHT_SET, jnp.float32)
    carried = jnp.asarray(VELOCITY_SET * WEIGHT_SET[:, None], jnp.float32)
    density = jnp.einsum('q,qxyz->xyz', weights, lattice, precision=HIGHEST)
    flux = jnp.einsum('qc,qxyz->cxyz', carried, lattice, precision=HIGHEST)
    return (density, flux / density)

def collide(lattice, density, velocity, force):
    shifted = velocity + RELAX_TIME * force / density
    along = jnp.einsum('qc,cxyz->qxyz', jnp.asarray(VELOCITY_SET, jnp.float32), shifted, precision=HIGHEST)
    square = lax.optimization_barrier(jnp.sum(shifted * shifted, axis=0))
    equilibrium = density * (1.0 + 3.0 * along + 4.5 * along * along - 1.5 * square)
    return lattice - (lattice - equilibrium) / RELAX_TIME

def stream_global(post):
    total_rows = post.shape[2]
    row_ids = jnp.arange(total_rows, dtype=jnp.int32)[None, :, None]
    moved_pops = []
    for number in range(19):
        offsets = tuple((int(component) for component in VELOCITY_SET[number]))
        rolled = jnp.roll(post[number], offsets, axis=(0, 1, 2))
        if number in FROM_BELOW:
            rolled = jnp.where(row_ids == 0, post[OPPOSITE[number]], rolled)
        if number in FROM_ABOVE:
            rolled = jnp.where(row_ids == total_rows - 1, post[OPPOSITE[number]], rolled)
        moved_pops.append(rolled)
    return jnp.stack(moved_pops)

def roll_pick(array, shift_x, shift_z):
    return jnp.roll(array, (-shift_x, -shift_z), axis=(-2, -1))

def bead_forces(places, speeds, kick_now, slot_state, far_places, far_speeds, far_kick, far_state, partner, occupied, drag_velocity, pick):
    capacity = places.shape[1]
    same_slot = jnp.eye(capacity, dtype=jnp.bool_)[:, :, None, None]
    totals = jnp.zeros_like(places)
    for shift_x in (-1, 0, 1):
        for shift_z in (-1, 0, 1):
            other_places = pick(far_places, shift_x, shift_z)
            other_speeds = pick(far_speeds, shift_x, shift_z)
            other_kick = pick(far_kick, shift_x, shift_z)
            other_state = pick(far_state, shift_x, shift_z)[None]
            offset = jnp.asarray([shift_x, 0.0, shift_z], jnp.float32).reshape(3, 1, 1, 1, 1)
            apart = places[:, :, None] - other_places[:, None] - offset
            dist_sq = lax.optimization_barrier(jnp.sum(apart * apart, axis=0))
            weight = jnp.maximum(1.0 - dist_sq, 0.0)
            closing = lax.optimization_barrier(jnp.sum(apart * (speeds[:, :, None] - other_speeds[:, None]), axis=0))
            own_state = slot_state[:, None]
            paired = (own_state < 2) & (other_state < 2)
            if shift_x == 0 and shift_z == 0:
                paired = paired & jnp.logical_not(same_slot)
            repel = jnp.where(own_state == other_state, REPEL_SAME, REPEL_CROSS)
            theta = (kick_now[:, None] + other_kick[None]) * HALF_ROOT
            strength = jnp.where(paired, repel * weight - FRICTION * weight * weight * closing + NOISE_SCALE * weight * theta, 0.0)
            totals = totals + lax.optimization_barrier(jnp.sum(strength[None] * apart, axis=2))
    slot_ids = jnp.arange(capacity, dtype=jnp.int32)[:, None, None, None]
    match = partner[None] == slot_ids
    partner_places = lax.optimization_barrier(jnp.sum(jnp.where(match[None], places[:, :, None], 0.0), axis=1))
    partner_alive = jnp.any(match & occupied[:, None], axis=0)
    bonded = occupied & partner_alive
    totals = totals + jnp.where(bonded[None], -BOND_STIFF * (places - partner_places), 0.0)
    totals = totals + DRAG_RATE * (drag_velocity[:, None] / VELOCITY_SCALE - speeds)
    return totals

def reference(populations, membrane_rows, positions, velocities, kicks, bead_types, bond_partner, tile_counts):
    density, velocity = moments(populations)
    row_ids = jnp.arange(NY, dtype=jnp.int32)[None, :, None]
    onehot = row_ids == membrane_rows[:, None, :]
    drag_velocity = lax.optimization_barrier(jnp.sum(jnp.where(onehot[None], velocity, 0.0), axis=2))
    push_force = jnp.asarray(PUSH_VECTOR, jnp.float32)[:, None, None, None]
    first_step = stream_global(collide(populations, density, velocity, push_force))

    def replica(bundle):
        places, speeds, kick_all, types_now, partner, counts_now = bundle
        capacity = places.shape[1]
        occupied = jnp.arange(capacity, dtype=jnp.int32)[:, None, None] < counts_now[None]
        slot_state = jnp.where(occupied, types_now, 2)
        for step_number in range(STEPS):
            kick_now = kick_all[step_number]
            totals = bead_forces(places, speeds, kick_now, slot_state, places, speeds, kick_now, slot_state, partner, occupied, drag_velocity, roll_pick)
            speeds = jnp.where(occupied[None], speeds + TIME_STEP * totals, 0.0)
            places = places + TIME_STEP * speeds
        places = jnp.where(occupied[None], places, 0.0)
        return (places, speeds, lax.optimization_barrier(jnp.sum(speeds, axis=1)), counts_now.astype(jnp.float32))
    new_places, new_speeds, speed_sums, counted = lax.map(replica, (positions, velocities, kicks, bead_types, bond_partner, tile_counts))
    cell_mean = lax.optimization_barrier(jnp.sum(speed_sums, axis=0)) / lax.optimization_barrier(jnp.sum(counted, axis=0))
    density, velocity = moments(first_step)
    force = jnp.where(onehot[None], COUPLE_RATE * (VELOCITY_SCALE * cell_mean[:, :, None, :] - velocity), 0.0) + push_force
    second = stream_global(collide(first_step, density, velocity, force))
    return (second, cell_mean, new_places, new_speeds)
```

```python
import math

import jax
import jax.numpy as jnp
import numpy as np
from jax import lax
from jax.experimental import pallas as pl
from jax.experimental.pallas import tpu as pltpu
from jax.sharding import PartitionSpec as P

VELOCITY_SET = (
    (0, 0, 0),
    (1, 0, 0),
    (-1, 0, 0),
    (0, 1, 0),
    (0, -1, 0),
    (0, 0, 1),
    (0, 0, -1),
    (1, 1, 0),
    (-1, -1, 0),
    (1, -1, 0),
    (-1, 1, 0),
    (1, 0, 1),
    (-1, 0, -1),
    (1, 0, -1),
    (-1, 0, 1),
    (0, 1, 1),
    (0, -1, -1),
    (0, 1, -1),
    (0, -1, 1),
)
WEIGHT_SET = (1.0 / 3.0,) + (1.0 / 18.0,) * 6 + (1.0 / 36.0,) * 12
OPPOSITE = (0, 2, 1, 4, 3, 6, 5, 8, 7, 10, 9, 12, 11, 14, 13, 16, 15, 18, 17)
Q = 19
TO_BRICK = ((1, 7, 9, 11, 13), (2, 8, 10, 12, 14))
TO_GROUP = ((3, 15, 17, 7, 10), (4, 16, 18, 9, 8))
RELAX_TIME = 0.8
PUSH = 0.001
VELOCITY_SCALE = 0.1
DRAG_RATE = 5.0
REPEL_SAME = 25.0
REPEL_CROSS = 50.0
FRICTION = 4.5
KICK_SCALE = 3.0 / math.sqrt(0.02) / math.sqrt(2.0)
TIME_STEP = 0.02
BOND_STIFF = 10.0
FAR = 1.0e8

GROUPS, BRICKS = 16, 32
CAP, NZ, LY, STEPS = 16, 128, 8, 3
MIDDLE = 7
MESH = pl.DeviceIdType.MESH
F32 = jnp.float32


def moments(g):
    def total(signs):
        parts = []
        for weight, members in ((1.0 / 18.0, range(1, 7)), (1.0 / 36.0, range(7, 19))):
            part = None
            for q in members:
                if signs[q]:
                    if part is None:
                        part = g[q] if signs[q] > 0 else -g[q]
                    else:
                        part = part + g[q] if signs[q] > 0 else part - g[q]
            parts.append(part * weight)
        return parts[0] + parts[1]

    density = g[0] * (1.0 / 3.0) + total((1,) * Q)
    inverse = 1.0 / density
    velocity = [total([c[axis] for c in VELOCITY_SET]) * inverse for axis in range(3)]
    return density, inverse, velocity


def along(q, s):
    value = None
    for axis in range(3):
        sign = VELOCITY_SET[q][axis]
        if sign:
            if value is None:
                value = s[axis] if sign > 0 else -s[axis]
            else:
                value = value + s[axis] if sign > 0 else value - s[axis]
    return value


def collide(g, density, inverse, velocity):
    s = [velocity[0] + (RELAX_TIME * PUSH) * inverse, velocity[1], velocity[2]]
    rest = 1.0 - 1.5 * (s[0] * s[0] + s[1] * s[1] + s[2] * s[2])
    post = []
    for q in range(Q):
        if q == 0:
            equilibrium = density * rest
        else:
            a = along(q, s)
            equilibrium = density * (rest + a * (3.0 + 4.5 * a))
        post.append(g[q] - (g[q] - equilibrium) * (1.0 / RELAX_TIME))
    return post


def kernel(
    pop_in,
    rows_in,
    pos_in,
    vel_in,
    kick_in,
    type_in,
    partner_in,
    count_in,
    pop_out,
    mean_out,
    pos_out,
    vel_out,
    cur,
    halo_kick,
    vel_send,
    halo_vel,
    near,
    drag,
    post,
    x_send,
    x_halo,
    row_send,
    row_halo,
    cells,
    sums,
    means,
    sem_cur,
    sem_kick,
    sem_vel,
    sem_drag,
    sem_x,
    sem_row,
    sem_cell,
    sem_sum,
    sem_mean,
):
    me_g = lax.axis_index("group")
    me_b = lax.axis_index("brick")
    up_b = lax.rem(me_b + 1, BRICKS)
    dn_b = lax.rem(me_b + BRICKS - 1, BRICKS)
    up_g = lax.rem(me_g + 1, GROUPS)
    dn_g = lax.rem(me_g + GROUPS - 1, GROUPS)
    is_mid = (me_g == MIDDLE) | (me_g == MIDDLE + 1)
    mid = jnp.where(me_g == MIDDLE, 0, 1)
    peers = [(lax.rem(me_g + k, GROUPS), me_b) for k in range(1, GROUPS)]
    beside = [(me_g, up_b), (me_g, dn_b)]
    corners = [(up_g, up_b), (up_g, dn_b), (dn_g, up_b), (dn_g, dn_b)]

    barrier = pltpu.get_barrier_semaphore()
    partners = peers + beside + corners
    for device in partners:
        pl.semaphore_signal(barrier, inc=1, device_id=device, device_id_type=MESH)

    unsent = []

    def remote(src, dst, send_sem, recv_sem, device):
        return pltpu.make_async_remote_copy(
            src_ref=src,
            dst_ref=dst,
            send_sem=send_sem,
            recv_sem=recv_sem,
            device_id=device,
            device_id_type=MESH,
        )

    def send(*args):
        copy = remote(*args)
        copy.start()
        unsent.append(copy)
        return copy

    row_ids = me_g * LY + lax.broadcasted_iota(jnp.int32, (LY, NZ), 0)
    at_cell = row_ids == rows_in[...]
    first_row = lax.broadcasted_iota(jnp.int32, (LY, NZ), 0) == 0
    last_row = lax.broadcasted_iota(jnp.int32, (LY, NZ), 0) == LY - 1
    low_wall = first_row & (me_g == 0)
    high_wall = last_row & (me_g == GROUPS - 1)

    slot_ids = lax.broadcasted_iota(jnp.int32, (CAP, NZ), 0)
    count = count_in[...]
    occupied = slot_ids < count
    tails = type_in[...].astype(F32)
    own_tail = type_in[...] == 1
    partner = partner_in[...]
    partner = jnp.where(partner < count, partner, slot_ids)
    cur[0, 0] = jnp.where(occupied, pos_in[0], FAR)
    cur[0, 1] = pos_in[1]
    cur[0, 2] = pos_in[2]
    for axis in range(3):
        cur[0, 3 + axis] = vel_in[axis]
    cur[0, 6] = kick_in[0]
    cur[0, 7] = tails

    g = [pop_in[q] for q in range(Q)]
    density, inverse, velocity = moments(g)

    @pl.when(is_mid)
    def _():
        for axis in range(3):
            drag[mid, axis : axis + 1, :] = jnp.sum(
                jnp.where(at_cell, velocity[axis], 0.0), axis=0, keepdims=True
            )

    def store_post(stage, values):
        for q in range(Q):
            post[stage, q] = values[q]
        for way in range(2):
            for n, q in enumerate(TO_BRICK[way]):
                x_send[stage, way, n] = values[q]
            edge = LY - 1 if way == 0 else 0
            for n, q in enumerate(TO_GROUP[way]):
                row_send[stage, way, n] = values[q][edge : edge + 1, :]

    store_post(0, collide(g, density, inverse, velocity))

    pl.semaphore_wait(barrier, len(partners))

    cur_copies = [
        send(cur.at[0], cur.at[2 - way], sem_cur.at[0, way], sem_cur.at[1, way], beside[way])
        for way in range(2)
    ]

    @pl.when(is_mid)
    def _():
        copies = [
            remote(drag.at[mid], drag.at[mid], sem_drag.at[k], sem_drag.at[16 + mid], peers[k])
            for k in range(GROUPS - 1)
        ]
        for copy in copies:
            copy.start()

    kick_copies = [
        send(
            kick_in.at[pl.ds(1, 2)],
            halo_kick.at[1 - way],
            sem_kick.at[0, way],
            sem_kick.at[1, way],
            beside[way],
        )
        for way in range(2)
    ]

    def send_post(stage):
        copies = []
        for way in range(2):
            copies.append(
                send(
                    x_send.at[stage, way],
                    x_halo.at[stage, way],
                    sem_x.at[0, stage, way],
                    sem_x.at[1, stage, way],
                    beside[way],
                )
            )
        for way in range(2):
            group = (up_g, dn_g)[way]
            for n, (start, size, brick) in enumerate(((0, 3, me_b), (3, 1, up_b), (4, 1, dn_b))):
                copies.append(
                    send(
                        row_send.at[stage, way, pl.ds(start, size)],
                        row_halo.at[stage, way, pl.ds(start, size)],
                        sem_row.at[0, stage, way, n],
                        sem_row.at[1, stage, way, n],
                        (group, brick),
                    )
                )
        return copies

    def stream(stage):
        moved = []
        for q in range(Q):
            cx, cy, cz = VELOCITY_SET[q]
            if cx == 0:
                value = post[stage, q]
            else:
                way = 0 if cx > 0 else 1
                value = x_halo[stage, way, TO_BRICK[way].index(q)]
            if cy:
                way = 0 if cy > 0 else 1
                edge = row_halo[stage, way, TO_GROUP[way].index(q)]
                value = pltpu.roll(value, 1 if cy > 0 else LY - 1, 0)
                value = jnp.where(first_row if cy > 0 else last_row, edge, value)
            if cz:
                value = pltpu.roll(value, 1 if cz > 0 else NZ - 1, 1)
            if cy:
                value = jnp.where(
                    low_wall if cy > 0 else high_wall, post[stage, OPPOSITE[q]], value
                )
            moved.append(value)
        return moved

    post_copies = send_post(0)

    def load_near(step, k):
        shift = (0.0, 1.0, -1.0)[k]
        places = [cur[k, axis] for axis in range(3)]
        if k == 0 or step == 0:
            speeds = [cur[k, 3 + axis] for axis in range(3)]
        else:
            speeds = [halo_vel[step - 1, k - 1, axis] for axis in range(3)]
            places = [p + TIME_STEP * v for p, v in zip(places, speeds)]
            if step < STEPS - 1:
                for axis in range(3):
                    cur[k, axis] = places[axis]
        if step == 0:
            kick = cur[k, 6]
        elif k == 0:
            kick = kick_in[step]
        else:
            kick = halo_kick[k - 1, step - 1]
        tail = cur[k, 7]
        push = KICK_SCALE * kick
        fields = [
            places[0] + shift,
            places[1],
            places[2],
            FRICTION * speeds[0],
            FRICTION * speeds[1],
            FRICTION * speeds[2],
            push + (REPEL_SAME + (REPEL_CROSS - REPEL_SAME) * tail),
            push + (REPEL_CROSS + (REPEL_SAME - REPEL_CROSS) * tail),
        ]
        for n, b in enumerate((-1, 0, 1)):
            for f, field in enumerate(fields):
                if b:
                    field = pltpu.roll(field, (-b) % NZ, 1)
                if f == 2:
                    field = field + float(b)
                near[n, f] = field

    def add_forces(step, totals):
        xi, yi, zi = [cur[0, axis] for axis in range(3)]
        ui, vi, wi = [FRICTION * cur[0, 3 + axis] for axis in range(3)]
        ki = KICK_SCALE * kick_in[step]

        def tile(n, totals):
            fx, fy, fz = totals
            for j in range(CAP):
                xj, yj, zj, uj, vj, wj, a0, a1 = [near[n, f, j : j + 1, :] for f in range(8)]
                dx = xi - xj
                dy = yi - yj
                dz = zi - zj
                weight = jnp.maximum(1.0 - (dx * dx + dy * dy + dz * dz), 0.0)
                closing = dx * (ui - uj) + dy * (vi - vj) + dz * (wi - wj)
                lift = jnp.where(own_tail, a1, a0) + ki
                strength = weight * (lift - weight * closing)
                fx = fx + strength * dx
                fy = fy + strength * dy
                fz = fz + strength * dz
            return fx, fy, fz

        return lax.fori_loop(0, 3, tile, totals)

    def bond_forces():
        places = [cur[0, axis] for axis in range(3)]
        found = list(places)
        for j in range(CAP):
            match = partner == j
            for axis in range(3):
                found[axis] = jnp.where(match, cur[0, axis, j : j + 1, :], found[axis])
        return tuple(-BOND_STIFF * (p - f) for p, f in zip(places, found))

    def cell_copies():
        other = MIDDLE + 1 - mid
        targets = [(other, me_b, 0), (me_g, up_b, 2), (other, up_b, 2)]
        targets += [(me_g, dn_b, 1), (other, dn_b, 1)]
        copies = []
        for n, (group, brick, column) in enumerate(targets):
            copies.append(
                remote(
                    cells.at[0, mid],
                    cells.at[column, mid],
                    sem_cell.at[n],
                    sem_cell.at[5 + 2 * column + mid],
                    (group, brick),
                )
            )
        return copies

    vel_copies = None
    for step in range(STEPS):
        totals = bond_forces()
        load_near(step, 0)
        totals = add_forces(step, totals)
        if step == 1:
            for copy in post_copies:
                copy.wait_recv()
            g = stream(0)
            density, inverse, velocity = moments(g)
            store_post(1, collide(g, density, inverse, velocity))
            post_copies = send_post(1)

            @pl.when(is_mid)
            def _():
                for n, value in enumerate([density] + velocity + [row_ids.astype(F32)]):
                    cells[0, mid, n : n + 1, :] = jnp.sum(
                        jnp.where(at_cell, value, 0.0), axis=0, keepdims=True
                    )
                for copy in cell_copies():
                    copy.start()

        if step == 2:
            for copy in post_copies:
                copy.wait_recv()
            g = stream(1)
            for q in range(Q):
                pop_out[q] = g[q]
        for k in (1, 2):
            if step == 0:
                cur_copies[2 - k].wait_recv()
            else:
                vel_copies[2 - k].wait_recv()
            if step == 1:
                kick_copies[2 - k].wait_recv()
            load_near(step, k)
            totals = add_forces(step, totals)
        if step == 0:
            for n in range(2):

                @pl.when(me_g != MIDDLE + n)
                def _():
                    remote(
                        drag.at[n], drag.at[n], sem_drag.at[0], sem_drag.at[16 + n], peers[0]
                    ).wait_recv()

            flow = (DRAG_RATE / VELOCITY_SCALE) * (drag[0, 0:3] + drag[1, 0:3])
            for copy in cur_copies:
                copy.wait_send()
        last = step == STEPS - 1
        for axis in range(3):
            speed = cur[0, 3 + axis]
            force = totals[axis] + (flow[axis : axis + 1] - DRAG_RATE * speed)
            speed = jnp.where(occupied, speed + TIME_STEP * force, 0.0)
            place = cur[0, axis] + TIME_STEP * speed
            if last:
                vel_out[axis] = speed
                pos_out[axis] = jnp.where(occupied, place, 0.0)
                sums[me_g, axis : axis + 1, :] = jnp.sum(speed, axis=0, keepdims=True)
            else:
                cur[0, 3 + axis] = speed
                cur[0, axis] = place
                vel_send[step, axis] = speed
        if last:
            sums[me_g, 3:4, :] = count.astype(F32)
        else:
            vel_copies = [
                send(
                    vel_send.at[step],
                    halo_vel.at[step, 1 - way],
                    sem_vel.at[0, step, way],
                    sem_vel.at[1, step, way],
                    beside[way],
                )
                for way in range(2)
            ]

    for k in range(GROUPS - 1):
        send(sums.at[me_g], sums.at[me_g], sem_sum.at[0, k], sem_sum.at[1, me_g], peers[k])
    for k in range(GROUPS - 1):
        other = peers[k][0]
        remote(
            sums.at[other], sums.at[other], sem_sum.at[0, k], sem_sum.at[1, other], peers[k]
        ).wait_recv()
    pooled = sums[0]
    for n in range(1, GROUPS):
        pooled = pooled + sums[n]
    mean = pooled[0:3] / pooled[3:4]
    mean_out[...] = mean

    @pl.when(is_mid)
    def _():
        means[2, 0:3] = mean
        mean_copies = [
            remote(means.at[2], means.at[1 - way], sem_mean.at[0, way], sem_mean.at[1, way], beside[way])
            for way in range(2)
        ]
        for copy in mean_copies:
            copy.start()
        for column in range(3):
            for n in range(2):
                wait = remote(
                    cells.at[0, mid],
                    cells.at[column, n],
                    sem_cell.at[0],
                    sem_cell.at[5 + 2 * column + n],
                    beside[0],
                )
                if column:
                    wait.wait_recv()
                else:

                    @pl.when(mid != n)
                    def _():
                        wait.wait_recv()

        def change(column, column_mean, members):
            cell = cells[column, 0] + cells[column, 1]
            density = cell[0:1]
            inverse = 1.0 / density
            row = cell[4:5].astype(jnp.int32)
            before, after = [], []
            for axis in range(3):
                speed = cell[1 + axis : 2 + axis]
                force = VELOCITY_SCALE * column_mean[axis : axis + 1] - speed
                pushed = speed + (RELAX_TIME * PUSH) * inverse if axis == 0 else speed
                before.append(pushed)
                after.append(pushed + RELAX_TIME * force * inverse)
            square = sum(a * a - b * b for a, b in zip(after, before))
            for q in members:
                cx, cy, cz = VELOCITY_SET[q]
                change = -1.5 * square
                if q:
                    a, b = along(q, after), along(q, before)
                    change = change + (a - b) * (3.0 + 4.5 * (a + b))
                change = (1.0 / RELAX_TIME) * density * change
                tile = jnp.where(row_ids == row + cy, change, 0.0)
                if cz:
                    tile = pltpu.roll(tile, 1 if cz > 0 else NZ - 1, 1)
                pop_out[q] += tile

        change(0, mean, [q for q in range(Q) if VELOCITY_SET[q][0] == 0])
        for way in range(2):
            mean_copies[way].wait_recv()
            change(2 - way, means[1 - way], TO_BRICK[way])
        for copy in mean_copies:
            copy.wait_send()
        for copy in cell_copies():
            copy.wait_send()
        for k in range(GROUPS - 1):
            remote(
                drag.at[mid], drag.at[mid], sem_drag.at[k], sem_drag.at[16 + mid], peers[k]
            ).wait_send()

    for copy in unsent:
        if not any(copy is other for other in cur_copies):
            copy.wait_send()


def local(
    populations, membrane_rows, positions, velocities, kicks, bead_types, bond_partner, tile_counts
):
    vmem = pl.BlockSpec(memory_space=pltpu.VMEM)
    dma = pltpu.SemaphoreType.DMA
    bead = (CAP, NZ)
    outs = pl.pallas_call(
        kernel,
        out_shape=(
            jax.ShapeDtypeStruct((Q, LY, NZ), F32),
            jax.ShapeDtypeStruct((3, NZ), F32),
            jax.ShapeDtypeStruct((3, *bead), F32),
            jax.ShapeDtypeStruct((3, *bead), F32),
        ),
        in_specs=[vmem] * 8,
        out_specs=[vmem] * 4,
        scratch_shapes=[
            pltpu.VMEM((3, 8, *bead), F32),
            pltpu.VMEM((2, 2, *bead), F32),
            pltpu.VMEM((2, 3, *bead), F32),
            pltpu.VMEM((2, 2, 3, *bead), F32),
            pltpu.VMEM((3, 8, *bead), F32),
            pltpu.VMEM((2, 8, NZ), F32),
            pltpu.VMEM((2, Q, LY, NZ), F32),
            pltpu.VMEM((2, 2, 5, LY, NZ), F32),
            pltpu.VMEM((2, 2, 5, LY, NZ), F32),
            pltpu.VMEM((2, 2, 5, 1, NZ), F32),
            pltpu.VMEM((2, 2, 5, 1, NZ), F32),
            pltpu.VMEM((3, 2, 8, NZ), F32),
            pltpu.VMEM((GROUPS, 4, NZ), F32),
            pltpu.VMEM((3, 8, NZ), F32),
            dma((2, 2)),
            dma((2, 2)),
            dma((2, 2, 2)),
            dma((18,)),
            dma((2, 2, 2)),
            dma((2, 2, 2, 3)),
            dma((11,)),
            dma((2, GROUPS)),
            dma((2, 2)),
        ],
        compiler_params=pltpu.CompilerParams(collective_id=0, has_side_effects=True),
        name="cycle",
    )(
        populations.reshape(Q, LY, NZ),
        membrane_rows,
        positions.reshape(3, *bead),
        velocities.reshape(3, *bead),
        kicks.reshape(STEPS, *bead),
        bead_types.reshape(bead),
        bond_partner.reshape(bead),
        tile_counts.reshape(1, NZ),
    )
    second, mean, places, speeds = outs
    return (
        second.reshape(Q, 1, LY, NZ),
        mean.reshape(3, 1, NZ),
        places.reshape(1, 3, CAP, 1, NZ),
        speeds.reshape(1, 3, CAP, 1, NZ),
    )


def solution(mesh):
    return jax.shard_map(
        local,
        mesh=mesh,
        in_specs=(
            P(None, "brick", "group", None),
            P("brick", None),
            P("group", None, None, "brick", None),
            P("group", None, None, "brick", None),
            P("group", None, None, "brick", None),
            P("group", None, "brick", None),
            P("group", None, "brick", None),
            P("group", "brick", None),
        ),
        out_specs=(
            P(None, "brick", "group", None),
            P(None, "brick", None),
            P("group", None, None, "brick", None),
            P("group", None, None, "brick", None),
        ),
        check_vma=False,
    )
```

```python
import math

import jax
import jax.numpy as jnp
import numpy as np
from jax import lax
from jax.experimental import pallas as pl
from jax.experimental.pallas import tpu as pltpu
from jax.sharding import PartitionSpec as P

VELOCITY_SET = (
    (0, 0, 0),
    (1, 0, 0),
    (-1, 0, 0),
    (0, 1, 0),
    (0, -1, 0),
    (0, 0, 1),
    (0, 0, -1),
    (1, 1, 0),
    (-1, -1, 0),
    (1, -1, 0),
    (-1, 1, 0),
    (1, 0, 1),
    (-1, 0, -1),
    (1, 0, -1),
    (-1, 0, 1),
    (0, 1, 1),
    (0, -1, -1),
    (0, 1, -1),
    (0, -1, 1),
)
WEIGHT_SET = (1.0 / 3.0,) + (1.0 / 18.0,) * 6 + (1.0 / 36.0,) * 12
OPPOSITE = (0, 2, 1, 4, 3, 6, 5, 8, 7, 10, 9, 12, 11, 14, 13, 16, 15, 18, 17)
Q = 19
TO_BRICK = ((1, 7, 9, 11, 13), (2, 8, 10, 12, 14))
TO_GROUP = ((3, 15, 17, 7, 10), (4, 16, 18, 9, 8))
RELAX_TIME = 0.8
PUSH = 0.001
VELOCITY_SCALE = 0.1
DRAG_RATE = 5.0
REPEL_SAME = 25.0
REPEL_CROSS = 50.0
FRICTION = 4.5
KICK_SCALE = 3.0 / math.sqrt(0.02) / math.sqrt(2.0)
TIME_STEP = 0.02
BOND_STIFF = 10.0
FAR = 1.0e8

GROUPS, BRICKS = 16, 32
CAP, NZ, LY, STEPS = 16, 128, 8, 3
MIDDLE = 7
MESH = pl.DeviceIdType.MESH
F32 = jnp.float32


def moments(g):
    def total(signs):
        parts = []
        for weight, members in ((1.0 / 18.0, range(1, 7)), (1.0 / 36.0, range(7, 19))):
            part = None
            for q in members:
                if signs[q]:
                    if part is None:
                        part = g[q] if signs[q] > 0 else -g[q]
                    else:
                        part = part + g[q] if signs[q] > 0 else part - g[q]
            parts.append(part * weight)
        return parts[0] + parts[1]

    density = g[0] * (1.0 / 3.0) + total((1,) * Q)
    inverse = 1.0 / density
    velocity = [total([c[axis] for c in VELOCITY_SET]) * inverse for axis in range(3)]
    return density, inverse, velocity


def along(q, s):
    value = None
    for axis in range(3):
        sign = VELOCITY_SET[q][axis]
        if sign:
            if value is None:
                value = s[axis] if sign > 0 else -s[axis]
            else:
                value = value + s[axis] if sign > 0 else value - s[axis]
    return value


def collide(g, density, inverse, velocity):
    s = [velocity[0] + (RELAX_TIME * PUSH) * inverse, velocity[1], velocity[2]]
    rest = 1.0 - 1.5 * (s[0] * s[0] + s[1] * s[1] + s[2] * s[2])
    post = []
    for q in range(Q):
        if q == 0:
            equilibrium = density * rest
        else:
            a = along(q, s)
            equilibrium = density * (rest + a * (3.0 + 4.5 * a))
        post.append(g[q] - (g[q] - equilibrium) * (1.0 / RELAX_TIME))
    return post


def kernel(
    pop_hbm,
    rows_hbm,
    pos_hbm,
    vel_hbm,
    kick_hbm,
    type_hbm,
    partner_hbm,
    count_hbm,
    pop_out,
    mean_out,
    pos_out,
    vel_out,
    pop_in,
    rows_in,
    pos_in,
    vel_in,
    kick_in,
    type_in,
    partner_in,
    count_in,
    sem_in,
    cur,
    halo_kick,
    vel_send,
    halo_vel,
    near,
    drag,
    post,
    x_send,
    x_halo,
    row_send,
    row_halo,
    cells,
    sums,
    means,
    sem_cur,
    sem_kick,
    sem_vel,
    sem_drag,
    sem_x,
    sem_row,
    sem_cell,
    sem_sum,
    sem_mean,
):
    me_g = lax.axis_index("group")
    me_b = lax.axis_index("brick")
    up_b = lax.rem(me_b + 1, BRICKS)
    dn_b = lax.rem(me_b + BRICKS - 1, BRICKS)
    up_g = lax.rem(me_g + 1, GROUPS)
    dn_g = lax.rem(me_g + GROUPS - 1, GROUPS)
    is_mid = (me_g == MIDDLE) | (me_g == MIDDLE + 1)
    mid = jnp.where(me_g == MIDDLE, 0, 1)
    peers = [(lax.rem(me_g + k, GROUPS), me_b) for k in range(1, GROUPS)]
    beside = [(me_g, up_b), (me_g, dn_b)]
    even = lax.rem(me_b, 2) == 0
    pair = [(me_g, jnp.where(even, up_b, dn_b)), (me_g, jnp.where(even, dn_b, up_b))]
    side = jnp.where(even, 1.0, -1.0)
    corners = [(up_g, up_b), (up_g, dn_b), (dn_g, up_b), (dn_g, dn_b)]

    barrier = pltpu.get_barrier_semaphore()
    partners = peers + beside + corners
    for device in partners:
        pl.semaphore_signal(barrier, inc=1, device_id=device, device_id_type=MESH)

    loads = {}
    for n, (name, source, target) in enumerate(
        (
            ("pos", pos_hbm, pos_in),
            ("vel", vel_hbm, vel_in),
            ("kick", kick_hbm, kick_in),
            ("type", type_hbm, type_in),
            ("count", count_hbm, count_in),
            ("partner", partner_hbm, partner_in),
            ("pop", pop_hbm, pop_in),
            ("rows", rows_hbm, rows_in),
        )
    ):
        loads[name] = pltpu.make_async_copy(source, target, sem_in.at[n])
        loads[name].start()

    unsent = []

    def remote(src, dst, send_sem, recv_sem, device):
        return pltpu.make_async_remote_copy(
            src_ref=src,
            dst_ref=dst,
            send_sem=send_sem,
            recv_sem=recv_sem,
            device_id=device,
            device_id_type=MESH,
        )

    def send(*args):
        copy = remote(*args)
        copy.start()
        unsent.append(copy)
        return copy

    for name in ("pos", "vel", "kick", "type", "count", "partner"):
        loads[name].wait()
    slot_ids = lax.broadcasted_iota(jnp.int32, (CAP, NZ), 0)
    count = count_in[...]
    occupied = slot_ids < count
    tails = type_in[...].astype(F32)
    own_tail = type_in[...] == 1
    partner = partner_in[...]
    partner = jnp.where(partner < count, partner, slot_ids)
    cur[0, 0] = jnp.where(occupied, pos_in[0], FAR)
    cur[0, 1] = pos_in[1]
    cur[0, 2] = pos_in[2]
    for axis in range(3):
        cur[0, 3 + axis] = vel_in[axis]
    cur[0, 6] = kick_in[0]
    cur[0, 7] = tails

    pl.semaphore_wait(barrier, len(partners))

    cur_copies = [
        send(cur.at[0], cur.at[1 + way], sem_cur.at[0, way], sem_cur.at[1, way], pair[way])
        for way in range(2)
    ]

    row_ids = me_g * LY + lax.broadcasted_iota(jnp.int32, (LY, NZ), 0)
    first_row = lax.broadcasted_iota(jnp.int32, (LY, NZ), 0) == 0
    last_row = lax.broadcasted_iota(jnp.int32, (LY, NZ), 0) == LY - 1
    low_wall = first_row & (me_g == 0)
    high_wall = last_row & (me_g == GROUPS - 1)

    for name in ("pop", "rows"):
        loads[name].wait()
    at_cell = row_ids == rows_in[...]
    g = [pop_in[q] for q in range(Q)]
    density, inverse, velocity = moments(g)

    @pl.when(is_mid)
    def _():
        for axis in range(3):
            drag[mid, axis : axis + 1, :] = jnp.sum(
                jnp.where(at_cell, velocity[axis], 0.0), axis=0, keepdims=True
            )

    def store_post(stage, values):
        for q in range(Q):
            post[stage, q] = values[q]
        for way in range(2):
            for n, q in enumerate(TO_BRICK[way]):
                x_send[stage, way, n] = values[q]
            edge = LY - 1 if way == 0 else 0
            for n, q in enumerate(TO_GROUP[way]):
                row_send[stage, way, n] = values[q][edge : edge + 1, :]

    store_post(0, collide(g, density, inverse, velocity))

    @pl.when(is_mid)
    def _():
        copies = [
            remote(drag.at[mid], drag.at[mid], sem_drag.at[k], sem_drag.at[16 + mid], peers[k])
            for k in range(GROUPS - 1)
        ]
        for copy in copies:
            copy.start()

    kick_copies = [
        send(
            kick_in.at[pl.ds(1, 2)],
            halo_kick.at[way],
            sem_kick.at[0, way],
            sem_kick.at[1, way],
            pair[way],
        )
        for way in range(2)
    ]

    def send_post(stage):
        copies = []
        for way in range(2):
            copies.append(
                send(
                    x_send.at[stage, way],
                    x_halo.at[stage, way],
                    sem_x.at[0, stage, way],
                    sem_x.at[1, stage, way],
                    beside[way],
                )
            )
        for way in range(2):
            group = (up_g, dn_g)[way]
            for n, (start, size, brick) in enumerate(((0, 3, me_b), (3, 1, up_b), (4, 1, dn_b))):
                copies.append(
                    send(
                        row_send.at[stage, way, pl.ds(start, size)],
                        row_halo.at[stage, way, pl.ds(start, size)],
                        sem_row.at[0, stage, way, n],
                        sem_row.at[1, stage, way, n],
                        (group, brick),
                    )
                )
        return copies

    def stream(stage):
        moved = []
        for q in range(Q):
            cx, cy, cz = VELOCITY_SET[q]
            if cx == 0:
                value = post[stage, q]
            else:
                way = 0 if cx > 0 else 1
                value = x_halo[stage, way, TO_BRICK[way].index(q)]
            if cy:
                way = 0 if cy > 0 else 1
                edge = row_halo[stage, way, TO_GROUP[way].index(q)]
                value = pltpu.roll(value, 1 if cy > 0 else LY - 1, 0)
                value = jnp.where(first_row if cy > 0 else last_row, edge, value)
            if cz:
                value = pltpu.roll(value, 1 if cz > 0 else NZ - 1, 1)
            if cy:
                value = jnp.where(
                    low_wall if cy > 0 else high_wall, post[stage, OPPOSITE[q]], value
                )
            moved.append(value)
        return moved

    post_copies = send_post(0)

    def load_near(step, k):
        shift = (0.0, side, -side)[k]
        places = [cur[k, axis] for axis in range(3)]
        if k == 0 or step == 0:
            speeds = [cur[k, 3 + axis] for axis in range(3)]
        else:
            speeds = [halo_vel[step - 1, k - 1, axis] for axis in range(3)]
            places = [p + TIME_STEP * v for p, v in zip(places, speeds)]
            if step < STEPS - 1:
                for axis in range(3):
                    cur[k, axis] = places[axis]
        if step == 0:
            kick = cur[k, 6]
        elif k == 0:
            kick = kick_in[step]
        else:
            kick = halo_kick[k - 1, step - 1]
        tail = cur[k, 7]
        push = KICK_SCALE * kick
        fields = [
            places[0] + shift,
            places[1],
            places[2],
            FRICTION * speeds[0],
            FRICTION * speeds[1],
            FRICTION * speeds[2],
            push + (REPEL_SAME + (REPEL_CROSS - REPEL_SAME) * tail),
            push + (REPEL_CROSS + (REPEL_SAME - REPEL_CROSS) * tail),
        ]
        for n, b in enumerate((-1, 0, 1)):
            for f, field in enumerate(fields):
                if b:
                    field = pltpu.roll(field, (-b) % NZ, 1)
                if f == 2:
                    field = field + float(b)
                near[n, f] = field

    def add_forces(step, totals):
        xi, yi, zi = [cur[0, axis] for axis in range(3)]
        ui, vi, wi = [FRICTION * cur[0, 3 + axis] for axis in range(3)]
        ki = KICK_SCALE * kick_in[step]

        def tile(n, totals):
            fx, fy, fz = totals
            for j in range(CAP):
                xj, yj, zj, uj, vj, wj, a0, a1 = [near[n, f, j : j + 1, :] for f in range(8)]
                dx = xi - xj
                dy = yi - yj
                dz = zi - zj
                weight = jnp.maximum(1.0 - (dx * dx + dy * dy + dz * dz), 0.0)
                closing = dx * (ui - uj) + dy * (vi - vj) + dz * (wi - wj)
                lift = jnp.where(own_tail, a1, a0) + ki
                strength = weight * (lift - weight * closing)
                fx = fx + strength * dx
                fy = fy + strength * dy
                fz = fz + strength * dz
            return fx, fy, fz

        return lax.fori_loop(0, 3, tile, totals)

    def bond_forces():
        places = [cur[0, axis] for axis in range(3)]
        found = list(places)
        for j in range(CAP):
            match = partner == j
            for axis in range(3):
                found[axis] = jnp.where(match, cur[0, axis, j : j + 1, :], found[axis])
        return tuple(-BOND_STIFF * (p - f) for p, f in zip(places, found))

    def cell_copies():
        other = MIDDLE + 1 - mid
        targets = [(other, me_b, 0), (me_g, up_b, 2), (other, up_b, 2)]
        targets += [(me_g, dn_b, 1), (other, dn_b, 1)]
        copies = []
        for n, (group, brick, column) in enumerate(targets):
            copies.append(
                remote(
                    cells.at[0, mid],
                    cells.at[column, mid],
                    sem_cell.at[n],
                    sem_cell.at[5 + 2 * column + mid],
                    (group, brick),
                )
            )
        return copies

    vel_copies = None
    for step in range(STEPS):
        totals = bond_forces()
        load_near(step, 0)
        totals = add_forces(step, totals)
        if step == 1:
            for copy in post_copies:
                copy.wait_recv()
            g = stream(0)
            density, inverse, velocity = moments(g)
            store_post(1, collide(g, density, inverse, velocity))
            post_copies = send_post(1)

            @pl.when(is_mid)
            def _():
                for n, value in enumerate([density] + velocity + [row_ids.astype(F32)]):
                    cells[0, mid, n : n + 1, :] = jnp.sum(
                        jnp.where(at_cell, value, 0.0), axis=0, keepdims=True
                    )
                for copy in cell_copies():
                    copy.start()

        if step == 2:
            for copy in post_copies:
                copy.wait_recv()
            g = stream(1)
            for q in range(Q):
                pop_out[q] = g[q]
        for k in (1, 2):
            if step == 0:
                cur_copies[k - 1].wait_recv()
            else:
                vel_copies[k - 1].wait_recv()
            if step == 1:
                kick_copies[k - 1].wait_recv()
            load_near(step, k)
            totals = add_forces(step, totals)
        if step == 0:
            for n in range(2):

                @pl.when(me_g != MIDDLE + n)
                def _():
                    remote(
                        drag.at[n], drag.at[n], sem_drag.at[0], sem_drag.at[16 + n], peers[0]
                    ).wait_recv()

            flow = (DRAG_RATE / VELOCITY_SCALE) * (drag[0, 0:3] + drag[1, 0:3])
            for copy in cur_copies:
                copy.wait_send()
        last = step == STEPS - 1
        for axis in range(3):
            speed = cur[0, 3 + axis]
            force = totals[axis] + (flow[axis : axis + 1] - DRAG_RATE * speed)
            speed = jnp.where(occupied, speed + TIME_STEP * force, 0.0)
            place = cur[0, axis] + TIME_STEP * speed
            if last:
                vel_out[axis] = speed
                pos_out[axis] = jnp.where(occupied, place, 0.0)
                sums[me_g, axis : axis + 1, :] = jnp.sum(speed, axis=0, keepdims=True)
            else:
                cur[0, 3 + axis] = speed
                cur[0, axis] = place
                vel_send[step, axis] = speed
        if last:
            sums[me_g, 3:4, :] = count.astype(F32)
        else:
            vel_copies = [
                send(
                    vel_send.at[step],
                    halo_vel.at[step, way],
                    sem_vel.at[0, step, way],
                    sem_vel.at[1, step, way],
                    pair[way],
                )
                for way in range(2)
            ]

    for k in range(GROUPS - 1):
        send(sums.at[me_g], sums.at[me_g], sem_sum.at[0, k], sem_sum.at[1, me_g], peers[k])
    for k in range(GROUPS - 1):
        other = peers[k][0]
        remote(
            sums.at[other], sums.at[other], sem_sum.at[0, k], sem_sum.at[1, other], peers[k]
        ).wait_recv()
    pooled = sums[0]
    for n in range(1, GROUPS):
        pooled = pooled + sums[n]
    mean = pooled[0:3] / pooled[3:4]
    for axis in range(3):
        mean_out[axis] = mean[axis : axis + 1]

    @pl.when(is_mid)
    def _():
        means[2, 0:3] = mean
        mean_copies = [
            remote(means.at[2], means.at[1 - way], sem_mean.at[0, way], sem_mean.at[1, way], beside[way])
            for way in range(2)
        ]
        for copy in mean_copies:
            copy.start()
        for column in range(3):
            for n in range(2):
                wait = remote(
                    cells.at[0, mid],
                    cells.at[column, n],
                    sem_cell.at[0],
                    sem_cell.at[5 + 2 * column + n],
                    beside[0],
                )
                if column:
                    wait.wait_recv()
                else:

                    @pl.when(mid != n)
                    def _():
                        wait.wait_recv()

        def change(column, column_mean, members):
            cell = cells[column, 0] + cells[column, 1]
            density = cell[0:1]
            inverse = 1.0 / density
            row = cell[4:5].astype(jnp.int32)
            before, after = [], []
            for axis in range(3):
                speed = cell[1 + axis : 2 + axis]
                force = VELOCITY_SCALE * column_mean[axis : axis + 1] - speed
                pushed = speed + (RELAX_TIME * PUSH) * inverse if axis == 0 else speed
                before.append(pushed)
                after.append(pushed + RELAX_TIME * force * inverse)
            square = sum(a * a - b * b for a, b in zip(after, before))
            for q in members:
                cx, cy, cz = VELOCITY_SET[q]
                change = -1.5 * square
                if q:
                    a, b = along(q, after), along(q, before)
                    change = change + (a - b) * (3.0 + 4.5 * (a + b))
                change = (1.0 / RELAX_TIME) * density * change
                tile = jnp.where(row_ids == row + cy, change, 0.0)
                if cz:
                    tile = pltpu.roll(tile, 1 if cz > 0 else NZ - 1, 1)
                pop_out[q] += tile

        change(0, mean, [q for q in range(Q) if VELOCITY_SET[q][0] == 0])
        for way in range(2):
            mean_copies[way].wait_recv()
            change(2 - way, means[1 - way], TO_BRICK[way])
        for copy in mean_copies:
            copy.wait_send()
        for copy in cell_copies():
            copy.wait_send()
        for k in range(GROUPS - 1):
            remote(
                drag.at[mid], drag.at[mid], sem_drag.at[k], sem_drag.at[16 + mid], peers[k]
            ).wait_send()

    for copy in unsent:
        if not any(copy is other for other in cur_copies):
            copy.wait_send()


def hand_out(*refs):
    sources, targets, sem = refs[:4], refs[4:8], refs[8]
    copies = [
        pltpu.make_async_copy(source, target, sem.at[n])
        for n, (source, target) in enumerate(zip(sources, targets))
    ]
    for copy in copies:
        copy.start()
    for copy in copies:
        copy.wait()


def local(
    populations, membrane_rows, positions, velocities, kicks, bead_types, bond_partner, tile_counts
):
    vmem = pl.BlockSpec(memory_space=pltpu.VMEM)
    hbm = pl.BlockSpec(memory_space=pltpu.HBM)
    anywhere = pl.BlockSpec(memory_space=pl.ANY)
    dma = pltpu.SemaphoreType.DMA
    bead = (CAP, NZ)
    outs = pl.pallas_call(
        kernel,
        out_shape=(
            pltpu.VMEM((Q, LY, NZ), F32),
            pltpu.VMEM((3, 1, NZ), F32),
            pltpu.VMEM((3, *bead), F32),
            pltpu.VMEM((3, *bead), F32),
        ),
        in_specs=[hbm] * 8,
        out_specs=[vmem] * 4,
        scratch_shapes=[
            pltpu.VMEM((Q, LY, NZ), F32),
            pltpu.VMEM((1, NZ), jnp.int32),
            pltpu.VMEM((3, *bead), F32),
            pltpu.VMEM((3, *bead), F32),
            pltpu.VMEM((STEPS, *bead), F32),
            pltpu.VMEM(bead, jnp.int32),
            pltpu.VMEM(bead, jnp.int32),
            pltpu.VMEM((1, NZ), jnp.int32),
            dma((8,)),
            pltpu.VMEM((3, 8, *bead), F32),
            pltpu.VMEM((2, 2, *bead), F32),
            pltpu.VMEM((2, 3, *bead), F32),
            pltpu.VMEM((2, 2, 3, *bead), F32),
            pltpu.VMEM((3, 8, *bead), F32),
            pltpu.VMEM((2, 8, NZ), F32),
            pltpu.VMEM((2, Q, LY, NZ), F32),
            pltpu.VMEM((2, 2, 5, LY, NZ), F32),
            pltpu.VMEM((2, 2, 5, LY, NZ), F32),
            pltpu.VMEM((2, 2, 5, 1, NZ), F32),
            pltpu.VMEM((2, 2, 5, 1, NZ), F32),
            pltpu.VMEM((3, 2, 8, NZ), F32),
            pltpu.VMEM((GROUPS, 4, NZ), F32),
            pltpu.VMEM((3, 8, NZ), F32),
            dma((2, 2)),
            dma((2, 2)),
            dma((2, 2, 2)),
            dma((18,)),
            dma((2, 2, 2)),
            dma((2, 2, 2, 3)),
            dma((11,)),
            dma((2, GROUPS)),
            dma((2, 2)),
        ],
        compiler_params=pltpu.CompilerParams(
            collective_id=0, has_side_effects=True, vmem_limit_bytes=4 << 20
        ),
        name="cycle",
    )(
        *(
            pltpu.with_memory_space_constraint(x, pltpu.HBM)
            for x in (
                populations.reshape(Q, LY, NZ),
                membrane_rows,
                positions.reshape(3, *bead),
                velocities.reshape(3, *bead),
                kicks.reshape(STEPS, *bead),
                bead_types.reshape(bead),
                bond_partner.reshape(bead),
                tile_counts.reshape(1, NZ),
            )
        )
    )
    second, mean, places, speeds = pl.pallas_call(
        hand_out,
        out_shape=tuple(jax.ShapeDtypeStruct(x.shape, F32) for x in outs),
        in_specs=[anywhere] * 4,
        out_specs=[hbm] * 4,
        scratch_shapes=[dma((4,))],
        compiler_params=pltpu.CompilerParams(vmem_limit_bytes=1 << 20),
        name="hand_out",
    )(*outs)
    return (
        second.reshape(Q, 1, LY, NZ),
        mean,
        places.reshape(1, 3, CAP, 1, NZ),
        speeds.reshape(1, 3, CAP, 1, NZ),
    )


def solution(mesh):
    return jax.shard_map(
        local,
        mesh=mesh,
        in_specs=(
            P(None, "brick", "group", None),
            P("brick", None),
            P("group", None, None, "brick", None),
            P("group", None, None, "brick", None),
            P("group", None, None, "brick", None),
            P("group", None, "brick", None),
            P("group", None, "brick", None),
            P("group", "brick", None),
        ),
        out_specs=(
            P(None, "brick", "group", None),
            P(None, "brick", None),
            P("group", None, None, "brick", None),
            P("group", None, None, "brick", None),
        ),
        check_vma=False,
    )
```

```python
import math

import jax
import jax.numpy as jnp
import numpy as np
from jax import lax
from jax.experimental import pallas as pl
from jax.experimental.pallas import tpu as pltpu
from jax.sharding import PartitionSpec as P

VELOCITY_SET = (
    (0, 0, 0),
    (1, 0, 0),
    (-1, 0, 0),
    (0, 1, 0),
    (0, -1, 0),
    (0, 0, 1),
    (0, 0, -1),
    (1, 1, 0),
    (-1, -1, 0),
    (1, -1, 0),
    (-1, 1, 0),
    (1, 0, 1),
    (-1, 0, -1),
    (1, 0, -1),
    (-1, 0, 1),
    (0, 1, 1),
    (0, -1, -1),
    (0, 1, -1),
    (0, -1, 1),
)
WEIGHT_SET = (1.0 / 3.0,) + (1.0 / 18.0,) * 6 + (1.0 / 36.0,) * 12
OPPOSITE = (0, 2, 1, 4, 3, 6, 5, 8, 7, 10, 9, 12, 11, 14, 13, 16, 15, 18, 17)
Q = 19
TO_BRICK = ((1, 7, 9, 11, 13), (2, 8, 10, 12, 14))
TO_GROUP = ((3, 15, 17, 7, 10), (4, 16, 18, 9, 8))
RELAX_TIME = 0.8
PUSH = 0.001
VELOCITY_SCALE = 0.1
DRAG_RATE = 5.0
REPEL_SAME = 25.0
REPEL_CROSS = 50.0
FRICTION = 4.5
KICK_SCALE = 3.0 / math.sqrt(0.02) / math.sqrt(2.0)
TIME_STEP = 0.02
BOND_STIFF = 10.0
FAR = 1.0e8

GROUPS, BRICKS = 16, 32
CAP, NZ, LY, STEPS = 16, 128, 8, 3
MIDDLE = 7
FARTHEST = (8, 7, 9, 6, 10, 5, 11, 4, 12, 3, 13, 2, 14, 1, 15)
MESH = pl.DeviceIdType.MESH
F32 = jnp.float32


def moments(g):
    def total(signs):
        parts = []
        for weight, members in ((1.0 / 18.0, range(1, 7)), (1.0 / 36.0, range(7, 19))):
            part = None
            for q in members:
                if signs[q]:
                    if part is None:
                        part = g[q] if signs[q] > 0 else -g[q]
                    else:
                        part = part + g[q] if signs[q] > 0 else part - g[q]
            parts.append(part * weight)
        return parts[0] + parts[1]

    density = g[0] * (1.0 / 3.0) + total((1,) * Q)
    inverse = 1.0 / density
    velocity = [total([c[axis] for c in VELOCITY_SET]) * inverse for axis in range(3)]
    return density, inverse, velocity


def along(q, s):
    value = None
    for axis in range(3):
        sign = VELOCITY_SET[q][axis]
        if sign:
            if value is None:
                value = s[axis] if sign > 0 else -s[axis]
            else:
                value = value + s[axis] if sign > 0 else value - s[axis]
    return value


def collide(g, density, inverse, velocity):
    s = [velocity[0] + (RELAX_TIME * PUSH) * inverse, velocity[1], velocity[2]]
    rest = 1.0 - 1.5 * (s[0] * s[0] + s[1] * s[1] + s[2] * s[2])
    post = []
    for q in range(Q):
        if q == 0:
            equilibrium = density * rest
        else:
            a = along(q, s)
            equilibrium = density * (rest + a * (3.0 + 4.5 * a))
        post.append(g[q] - (g[q] - equilibrium) * (1.0 / RELAX_TIME))
    return post


def kernel(
    pop_hbm,
    rows_hbm,
    pos_hbm,
    vel_hbm,
    kick_hbm,
    type_hbm,
    partner_hbm,
    count_hbm,
    pop_out,
    mean_out,
    pos_out,
    vel_out,
    pop_in,
    rows_in,
    pos_in,
    vel_in,
    kick_in,
    type_in,
    partner_in,
    count_in,
    sem_in,
    cur,
    halo_kick,
    vel_send,
    halo_vel,
    near,
    drag,
    post,
    x_send,
    x_halo,
    row_send,
    row_halo,
    cells,
    sums,
    means,
    sem_cur,
    sem_kick,
    sem_vel,
    sem_drag,
    sem_x,
    sem_row,
    sem_cell,
    sem_sum,
    sem_mean,
    sem_entered,
    sem_ready,
):
    me_g = lax.axis_index("group")
    me_b = lax.axis_index("brick")
    up_b = lax.rem(me_b + 1, BRICKS)
    dn_b = lax.rem(me_b + BRICKS - 1, BRICKS)
    up_g = lax.rem(me_g + 1, GROUPS)
    dn_g = lax.rem(me_g + GROUPS - 1, GROUPS)
    is_mid = (me_g == MIDDLE) | (me_g == MIDDLE + 1)
    mid = jnp.where(me_g == MIDDLE, 0, 1)
    peers = [(lax.rem(me_g + k, GROUPS), me_b) for k in range(1, GROUPS)]
    beside = [(me_g, up_b), (me_g, dn_b)]
    even = lax.rem(me_b, 2) == 0
    pair = [(me_g, jnp.where(even, up_b, dn_b)), (me_g, jnp.where(even, dn_b, up_b))]
    side = jnp.where(even, 1.0, -1.0)
    corners = [(up_g, up_b), (up_g, dn_b), (dn_g, up_b), (dn_g, dn_b)]

    far_mids = [(MIDDLE, pair[1][1]), (MIDDLE + 1, pair[1][1])]

    loads = {}
    for n, (name, source, target) in enumerate(
        (
            ("pos", pos_hbm, pos_in),
            ("vel", vel_hbm, vel_in),
            ("kick", kick_hbm, kick_in),
            ("type", type_hbm, type_in),
            ("count", count_hbm, count_in),
            ("pop", pop_hbm, pop_in),
            ("rows", rows_hbm, rows_in),
            ("partner", partner_hbm, partner_in),
        )
    ):
        loads[name] = pltpu.make_async_copy(source, target, sem_in.at[n])
        loads[name].start()

    barrier = pltpu.get_barrier_semaphore()
    partners = pair[::-1] + [peers[k - 1] for k in FARTHEST] + corners
    for device in partners:
        pl.semaphore_signal(barrier, inc=1, device_id=device, device_id_type=MESH)

    unsent = []

    def remote(src, dst, send_sem, recv_sem, device):
        return pltpu.make_async_remote_copy(
            src_ref=src,
            dst_ref=dst,
            send_sem=send_sem,
            recv_sem=recv_sem,
            device_id=device,
            device_id_type=MESH,
        )

    def send(*args):
        copy = remote(*args)
        copy.start()
        unsent.append(copy)
        return copy

    for name in ("pos", "vel", "kick", "type", "count"):
        loads[name].wait()
    slot_ids = lax.broadcasted_iota(jnp.int32, (CAP, NZ), 0)
    count = count_in[...]
    occupied = slot_ids < count
    tails = type_in[...].astype(F32)
    own_tail = type_in[...] == 1
    cur[0, 0] = jnp.where(occupied, pos_in[0], FAR)
    cur[0, 1] = pos_in[1]
    cur[0, 2] = pos_in[2]
    for axis in range(3):
        cur[0, 3 + axis] = vel_in[axis]
    cur[0, 6] = kick_in[0]
    cur[0, 7] = tails

    pl.semaphore_wait(barrier, len(partners))

    @pl.when(is_mid)
    def _():
        pl.semaphore_signal(sem_entered, inc=1, device_id=pair[1], device_id_type=MESH)

    def send_pair(source, target, sems):
        copies = [
            send(source, target.at[way], sems.at[0, way], sems.at[1, way], pair[way])
            for way in (1, 0)
        ]
        return copies[::-1]

    cur_copies = send_pair(cur.at[0], cur.at[pl.ds(1, 2)], sem_cur)

    row_ids = me_g * LY + lax.broadcasted_iota(jnp.int32, (LY, NZ), 0)
    first_row = lax.broadcasted_iota(jnp.int32, (LY, NZ), 0) == 0
    last_row = lax.broadcasted_iota(jnp.int32, (LY, NZ), 0) == LY - 1
    low_wall = first_row & (me_g == 0)
    high_wall = last_row & (me_g == GROUPS - 1)

    for name in ("pop", "rows"):
        loads[name].wait()
    at_cell = row_ids == rows_in[...]
    g = [pop_in[q] for q in range(Q)]
    density, inverse, velocity = moments(g)

    def drag_copies():
        return [
            remote(drag.at[mid], drag.at[mid], sem_drag.at[k - 1], sem_drag.at[16 + mid], peers[k - 1])
            for k in FARTHEST
        ]

    @pl.when(is_mid)
    def _():
        for axis in range(3):
            drag[mid, axis : axis + 1, :] = jnp.sum(
                jnp.where(at_cell, velocity[axis], 0.0), axis=0, keepdims=True
            )
        for copy in drag_copies():
            copy.start()

    kick_copies = send_pair(kick_in.at[pl.ds(1, 2)], halo_kick, sem_kick)

    def store_post(stage, values):
        for q in range(Q):
            post[stage, q] = values[q]
        for way in range(2):
            for n, q in enumerate(TO_BRICK[way]):
                x_send[stage, way, n] = values[q]
            edge = LY - 1 if way == 0 else 0
            for n, q in enumerate(TO_GROUP[way]):
                row_send[stage, way, n] = values[q][edge : edge + 1, :]

    store_post(0, collide(g, density, inverse, velocity))

    def send_post(stage):
        copies = []
        for way in range(2):
            copies.append(
                send(
                    x_send.at[stage, way],
                    x_halo.at[stage, way],
                    sem_x.at[0, stage, way],
                    sem_x.at[1, stage, way],
                    beside[way],
                )
            )
        for way in range(2):
            group = (up_g, dn_g)[way]
            for n, (start, size, brick) in enumerate(((0, 3, me_b), (3, 1, up_b), (4, 1, dn_b))):
                copies.append(
                    send(
                        row_send.at[stage, way, pl.ds(start, size)],
                        row_halo.at[stage, way, pl.ds(start, size)],
                        sem_row.at[0, stage, way, n],
                        sem_row.at[1, stage, way, n],
                        (group, brick),
                    )
                )
        return copies

    def stream(stage):
        moved = []
        for q in range(Q):
            cx, cy, cz = VELOCITY_SET[q]
            if cx == 0:
                value = post[stage, q]
            else:
                way = 0 if cx > 0 else 1
                value = x_halo[stage, way, TO_BRICK[way].index(q)]
            if cy:
                way = 0 if cy > 0 else 1
                edge = row_halo[stage, way, TO_GROUP[way].index(q)]
                value = pltpu.roll(value, 1 if cy > 0 else LY - 1, 0)
                value = jnp.where(first_row if cy > 0 else last_row, edge, value)
            if cz:
                value = pltpu.roll(value, 1 if cz > 0 else NZ - 1, 1)
            if cy:
                value = jnp.where(
                    low_wall if cy > 0 else high_wall, post[stage, OPPOSITE[q]], value
                )
            moved.append(value)
        return moved

    post_copies = send_post(0)

    def load_near(step, k):
        shift = (0.0, side, -side)[k]
        places = [cur[k, axis] for axis in range(3)]
        if k == 0 or step == 0:
            speeds = [cur[k, 3 + axis] for axis in range(3)]
        else:
            speeds = [halo_vel[step - 1, k - 1, axis] for axis in range(3)]
            places = [p + TIME_STEP * v for p, v in zip(places, speeds)]
            if step < STEPS - 1:
                for axis in range(3):
                    cur[k, axis] = places[axis]
        if step == 0:
            kick = cur[k, 6]
        elif k == 0:
            kick = kick_in[step]
        else:
            kick = halo_kick[k - 1, step - 1]
        tail = cur[k, 7]
        push = KICK_SCALE * kick
        fields = [
            places[0] + shift,
            places[1],
            places[2],
            FRICTION * speeds[0],
            FRICTION * speeds[1],
            FRICTION * speeds[2],
            push + (REPEL_SAME + (REPEL_CROSS - REPEL_SAME) * tail),
            push + (REPEL_CROSS + (REPEL_SAME - REPEL_CROSS) * tail),
        ]
        for n, b in enumerate((-1, 0, 1)):
            for f, field in enumerate(fields):
                if b:
                    field = pltpu.roll(field, (-b) % NZ, 1)
                if f == 2:
                    field = field + float(b)
                near[n, f] = field

    def add_forces(step, totals):
        xi, yi, zi = [cur[0, axis] for axis in range(3)]
        ui, vi, wi = [FRICTION * cur[0, 3 + axis] for axis in range(3)]
        ki = KICK_SCALE * kick_in[step]

        def tile(n, totals):
            fx, fy, fz = totals
            for j in range(CAP):
                xj, yj, zj, uj, vj, wj, a0, a1 = [near[n, f, j : j + 1, :] for f in range(8)]
                dx = xi - xj
                dy = yi - yj
                dz = zi - zj
                weight = jnp.maximum(1.0 - (dx * dx + dy * dy + dz * dz), 0.0)
                closing = dx * (ui - uj) + dy * (vi - vj) + dz * (wi - wj)
                lift = jnp.where(own_tail, a1, a0) + ki
                strength = weight * (lift - weight * closing)
                fx = fx + strength * dx
                fy = fy + strength * dy
                fz = fz + strength * dz
            return fx, fy, fz

        for n in range(3):
            totals = tile(n, totals)
        return totals

    loads["partner"].wait()
    partner = partner_in[...]
    partner = jnp.where(partner < count, partner, slot_ids)

    def bond_forces():
        places = [cur[0, axis] for axis in range(3)]
        found = list(places)
        for j in range(CAP):
            match = partner == j
            for axis in range(3):
                found[axis] = jnp.where(match, cur[0, axis, j : j + 1, :], found[axis])
        return tuple(-BOND_STIFF * (p - f) for p, f in zip(places, found))

    def cell_copies():
        other = MIDDLE + 1 - mid
        targets = [(other, me_b, 0), (me_g, up_b, 2), (other, up_b, 2)]
        targets += [(me_g, dn_b, 1), (other, dn_b, 1)]
        copies = []
        for n, (group, brick, column) in enumerate(targets):
            copies.append(
                remote(
                    cells.at[0, mid],
                    cells.at[column, mid],
                    sem_cell.at[n],
                    sem_cell.at[5 + 2 * column + mid],
                    (group, brick),
                )
            )
        return copies

    def lattice_between():
        for copy in post_copies:
            copy.wait_recv()
        g = stream(0)
        density, inverse, velocity = moments(g)
        store_post(1, collide(g, density, inverse, velocity))
        copies = send_post(1)

        @pl.when(is_mid)
        def _():
            pl.semaphore_wait(sem_entered, 1)
            for n in range(GROUPS):
                pl.semaphore_signal(
                    sem_ready, inc=1, device_id=(n, pair[1][1]), device_id_type=MESH
                )
            for n, value in enumerate([density] + velocity + [row_ids.astype(F32)]):
                cells[0, mid, n : n + 1, :] = jnp.sum(
                    jnp.where(at_cell, value, 0.0), axis=0, keepdims=True
                )
            for copy in cell_copies():
                copy.start()

        return copies

    moving = cur_copies
    for step in range(STEPS):
        totals = bond_forces()
        load_near(step, 0)
        totals = add_forces(step, totals)
        for k in (1, 2):
            if step == 1 and k == 2:
                post_copies = lattice_between()
            moving[k - 1].wait_recv()
            if step == 1:
                kick_copies[k - 1].wait_recv()
            load_near(step, k)
            totals = add_forces(step, totals)
        if step == 0:
            for n in range(2):

                @pl.when(me_g != MIDDLE + n)
                def _():
                    remote(
                        drag.at[n], drag.at[n], sem_drag.at[0], sem_drag.at[16 + n], peers[0]
                    ).wait_recv()

            flow = (DRAG_RATE / VELOCITY_SCALE) * (drag[0, 0:3] + drag[1, 0:3])
            for copy in cur_copies:
                copy.wait_send()
        last = step == STEPS - 1
        for axis in range(3):
            speed = cur[0, 3 + axis]
            force = totals[axis] + (flow[axis : axis + 1] - DRAG_RATE * speed)
            speed = jnp.where(occupied, speed + TIME_STEP * force, 0.0)
            if last:
                vel_out[axis] = speed
                sums[0, me_g, axis : axis + 1, :] = jnp.sum(speed, axis=0, keepdims=True)
            else:
                cur[0, 3 + axis] = speed
                vel_send[step, axis] = speed
        if not last:
            moving = send_pair(vel_send.at[step], halo_vel.at[step], sem_vel.at[step])
            for axis in range(3):
                cur[0, axis] += TIME_STEP * cur[0, 3 + axis]

    sums[0, me_g, 3:4, :] = count.astype(F32)
    for k in FARTHEST:
        send(
            sums.at[0, me_g], sums.at[0, me_g], sem_sum.at[k - 1], sem_sum.at[17 + me_g], peers[k - 1]
        )
    pl.semaphore_wait(sem_ready, len(far_mids))
    for n in range(2):
        send(sums.at[0, me_g], sums.at[1, me_g], sem_sum.at[15 + n], sem_sum.at[33 + me_g], far_mids[n])

    for axis in range(3):
        pos_out[axis] = jnp.where(occupied, cur[0, axis] + TIME_STEP * vel_out[axis], 0.0)
    for copy in post_copies:
        copy.wait_recv()
    g = stream(1)
    for q in range(Q):
        pop_out[q] = g[q]

    def wait_sums(which, others):
        for other in others:
            remote(
                sums.at[which, other],
                sums.at[which, other],
                sem_sum.at[0],
                sem_sum.at[17 + 16 * which + other],
                peers[0],
            ).wait_recv()

    def pooled(which):
        total = sums[which, 0]
        for n in range(1, GROUPS):
            total = total + sums[which, n]
        return total[0:3] / total[3:4]

    wait_sums(0, [peers[k - 1][0] for k in reversed(FARTHEST)])
    mean = pooled(0)
    for axis in range(3):
        mean_out[axis] = mean[axis : axis + 1]

    @pl.when(is_mid)
    def _():
        means[2, 0:3] = mean
        mean_copy = remote(means.at[2], means.at[0], sem_mean.at[0], sem_mean.at[1], pair[0])
        mean_copy.start()
        for column in range(3):
            for n in range(2):
                wait = remote(
                    cells.at[0, mid],
                    cells.at[column, n],
                    sem_cell.at[0],
                    sem_cell.at[5 + 2 * column + n],
                    beside[0],
                )
                if column:
                    wait.wait_recv()
                else:

                    @pl.when(mid != n)
                    def _():
                        wait.wait_recv()

        def change(column, column_mean, members):
            cell = cells[column, 0] + cells[column, 1]
            density = cell[0:1]
            inverse = 1.0 / density
            row = cell[4:5].astype(jnp.int32)
            before, after = [], []
            for axis in range(3):
                speed = cell[1 + axis : 2 + axis]
                force = VELOCITY_SCALE * column_mean[axis : axis + 1] - speed
                pushed = speed + (RELAX_TIME * PUSH) * inverse if axis == 0 else speed
                before.append(pushed)
                after.append(pushed + RELAX_TIME * force * inverse)
            square = sum(a * a - b * b for a, b in zip(after, before))
            for q in members:
                cx, cy, cz = VELOCITY_SET[q]
                change = -1.5 * square
                if q:
                    a, b = along(q, after), along(q, before)
                    change = change + (a - b) * (3.0 + 4.5 * (a + b))
                change = (1.0 / RELAX_TIME) * density * change
                tile = jnp.where(row_ids == row + cy, change, 0.0)
                if cz:
                    tile = pltpu.roll(tile, 1 if cz > 0 else NZ - 1, 1)
                pop_out[q] += tile

        change(0, mean, [q for q in range(Q) if VELOCITY_SET[q][0] == 0])
        mean_copy.wait_recv()
        wait_sums(1, range(GROUPS))
        far_mean = pooled(1)
        near_mean = means[0, 0:3]
        change(1, jnp.where(even, near_mean, far_mean), TO_BRICK[1])
        change(2, jnp.where(even, far_mean, near_mean), TO_BRICK[0])
        mean_copy.wait_send()
        for copy in cell_copies():
            copy.wait_send()
        for copy in drag_copies():
            copy.wait_send()

    for copy in unsent:
        if not any(copy is other for other in cur_copies):
            copy.wait_send()


def hand_out(*refs):
    sources, targets, sem = refs[:4], refs[4:8], refs[8]
    copies = [
        pltpu.make_async_copy(source, target, sem.at[n])
        for n, (source, target) in enumerate(zip(sources, targets))
    ]
    for copy in copies:
        copy.start()
    for copy in copies:
        copy.wait()


def local(
    populations, membrane_rows, positions, velocities, kicks, bead_types, bond_partner, tile_counts
):
    vmem = pl.BlockSpec(memory_space=pltpu.VMEM)
    hbm = pl.BlockSpec(memory_space=pltpu.HBM)
    anywhere = pl.BlockSpec(memory_space=pl.ANY)
    dma = pltpu.SemaphoreType.DMA
    bead = (CAP, NZ)
    outs = pl.pallas_call(
        kernel,
        out_shape=(
            pltpu.VMEM((Q, LY, NZ), F32),
            pltpu.VMEM((3, 1, NZ), F32),
            pltpu.VMEM((3, *bead), F32),
            pltpu.VMEM((3, *bead), F32),
        ),
        in_specs=[hbm] * 8,
        out_specs=[vmem] * 4,
        scratch_shapes=[
            pltpu.VMEM((Q, LY, NZ), F32),
            pltpu.VMEM((1, NZ), jnp.int32),
            pltpu.VMEM((3, *bead), F32),
            pltpu.VMEM((3, *bead), F32),
            pltpu.VMEM((STEPS, *bead), F32),
            pltpu.VMEM(bead, jnp.int32),
            pltpu.VMEM(bead, jnp.int32),
            pltpu.VMEM((1, NZ), jnp.int32),
            dma((8,)),
            pltpu.VMEM((3, 8, *bead), F32),
            pltpu.VMEM((2, 2, *bead), F32),
            pltpu.VMEM((2, 3, *bead), F32),
            pltpu.VMEM((2, 2, 3, *bead), F32),
            pltpu.VMEM((3, 8, *bead), F32),
            pltpu.VMEM((2, 8, NZ), F32),
            pltpu.VMEM((2, Q, LY, NZ), F32),
            pltpu.VMEM((2, 2, 5, LY, NZ), F32),
            pltpu.VMEM((2, 2, 5, LY, NZ), F32),
            pltpu.VMEM((2, 2, 5, 1, NZ), F32),
            pltpu.VMEM((2, 2, 5, 1, NZ), F32),
            pltpu.VMEM((3, 2, 8, NZ), F32),
            pltpu.VMEM((2, GROUPS, 4, NZ), F32),
            pltpu.VMEM((3, 8, NZ), F32),
            dma((2, 2)),
            dma((2, 2)),
            dma((2, 2, 2)),
            dma((18,)),
            dma((2, 2, 2)),
            dma((2, 2, 2, 3)),
            dma((11,)),
            dma((49,)),
            dma((2,)),
            pltpu.SemaphoreType.REGULAR,
            pltpu.SemaphoreType.REGULAR,
        ],
        compiler_params=pltpu.CompilerParams(
            collective_id=0, has_side_effects=True, vmem_limit_bytes=4 << 20
        ),
        name="cycle",
    )(
        *(
            pltpu.with_memory_space_constraint(x, pltpu.HBM)
            for x in (
                populations.reshape(Q, LY, NZ),
                membrane_rows,
                positions.reshape(3, *bead),
                velocities.reshape(3, *bead),
                kicks.reshape(STEPS, *bead),
                bead_types.reshape(bead),
                bond_partner.reshape(bead),
                tile_counts.reshape(1, NZ),
            )
        )
    )
    second, mean, places, speeds = pl.pallas_call(
        hand_out,
        out_shape=tuple(jax.ShapeDtypeStruct(x.shape, F32) for x in outs),
        in_specs=[anywhere] * 4,
        out_specs=[hbm] * 4,
        scratch_shapes=[dma((4,))],
        compiler_params=pltpu.CompilerParams(vmem_limit_bytes=1 << 20),
        name="hand_out",
    )(*outs)
    return (
        second.reshape(Q, 1, LY, NZ),
        mean,
        places.reshape(1, 3, CAP, 1, NZ),
        speeds.reshape(1, 3, CAP, 1, NZ),
    )


def solution(mesh):
    return jax.shard_map(
        local,
        mesh=mesh,
        in_specs=(
            P(None, "brick", "group", None),
            P("brick", None),
            P("group", None, None, "brick", None),
            P("group", None, None, "brick", None),
            P("group", None, None, "brick", None),
            P("group", None, "brick", None),
            P("group", None, "brick", None),
            P("group", "brick", None),
        ),
        out_specs=(
            P(None, "brick", "group", None),
            P(None, "brick", None),
            P("group", None, None, "brick", None),
            P("group", None, None, "brick", None),
        ),
        check_vma=False,
    )
```

```python
import math

import jax
import jax.numpy as jnp
import numpy as np
from jax import lax
from jax.experimental import pallas as pl
from jax.experimental.pallas import tpu as pltpu
from jax.sharding import PartitionSpec as P

VELOCITY_SET = (
    (0, 0, 0),
    (1, 0, 0),
    (-1, 0, 0),
    (0, 1, 0),
    (0, -1, 0),
    (0, 0, 1),
    (0, 0, -1),
    (1, 1, 0),
    (-1, -1, 0),
    (1, -1, 0),
    (-1, 1, 0),
    (1, 0, 1),
    (-1, 0, -1),
    (1, 0, -1),
    (-1, 0, 1),
    (0, 1, 1),
    (0, -1, -1),
    (0, 1, -1),
    (0, -1, 1),
)
WEIGHT_SET = (1.0 / 3.0,) + (1.0 / 18.0,) * 6 + (1.0 / 36.0,) * 12
OPPOSITE = (0, 2, 1, 4, 3, 6, 5, 8, 7, 10, 9, 12, 11, 14, 13, 16, 15, 18, 17)
Q = 19
TO_BRICK = ((1, 7, 9, 11, 13), (2, 8, 10, 12, 14))
TO_GROUP = ((3, 15, 17, 7, 10), (4, 16, 18, 9, 8))
RELAX_TIME = 0.8
PUSH = 0.001
VELOCITY_SCALE = 0.1
DRAG_RATE = 5.0
REPEL_SAME = 25.0
REPEL_CROSS = 50.0
FRICTION = 4.5
KICK_SCALE = 3.0 / math.sqrt(0.02) / math.sqrt(2.0)
TIME_STEP = 0.02
BOND_STIFF = 10.0
FAR = 1.0e8

GROUPS, BRICKS = 16, 32
CAP, NZ, LY, STEPS = 16, 128, 8, 3
MIDDLE = 7
FARTHEST = (8, 7, 9, 6, 10, 5, 11, 4, 12, 3, 13, 2, 14, 1, 15)
MESH = pl.DeviceIdType.MESH
F32 = jnp.float32


def moments(g):
    def total(signs):
        parts = []
        for weight, members in ((1.0 / 18.0, range(1, 7)), (1.0 / 36.0, range(7, 19))):
            part = None
            for q in members:
                if signs[q]:
                    if part is None:
                        part = g[q] if signs[q] > 0 else -g[q]
                    else:
                        part = part + g[q] if signs[q] > 0 else part - g[q]
            parts.append(part * weight)
        return parts[0] + parts[1]

    density = g[0] * (1.0 / 3.0) + total((1,) * Q)
    inverse = 1.0 / density
    velocity = [total([c[axis] for c in VELOCITY_SET]) * inverse for axis in range(3)]
    return density, inverse, velocity


def along(q, s):
    value = None
    for axis in range(3):
        sign = VELOCITY_SET[q][axis]
        if sign:
            if value is None:
                value = s[axis] if sign > 0 else -s[axis]
            else:
                value = value + s[axis] if sign > 0 else value - s[axis]
    return value


def collide(g, density, inverse, velocity):
    s = [velocity[0] + (RELAX_TIME * PUSH) * inverse, velocity[1], velocity[2]]
    rest = 1.0 - 1.5 * (s[0] * s[0] + s[1] * s[1] + s[2] * s[2])
    post = []
    for q in range(Q):
        if q == 0:
            equilibrium = density * rest
        else:
            a = along(q, s)
            equilibrium = density * (rest + a * (3.0 + 4.5 * a))
        post.append(g[q] - (g[q] - equilibrium) * (1.0 / RELAX_TIME))
    return post


def kernel(
    pop_hbm,
    rows_hbm,
    pos_hbm,
    vel_hbm,
    kick_hbm,
    type_hbm,
    partner_hbm,
    count_hbm,
    pop_out,
    mean_out,
    pos_out,
    vel_out,
    pop_in,
    rows_in,
    pos_in,
    vel_in,
    kick_in,
    type_in,
    partner_in,
    count_in,
    sem_in,
    cur,
    halo_kick,
    vel_send,
    halo_vel,
    near,
    drag,
    post,
    x_send,
    x_halo,
    row_send,
    row_halo,
    cells,
    sums,
    means,
    sem_cur,
    sem_kick,
    sem_vel,
    sem_drag,
    sem_x,
    sem_row,
    sem_cell,
    sem_sum,
    sem_mean,
    sem_entered,
    sem_ready,
):
    me_g = lax.axis_index("group")
    me_b = lax.axis_index("brick")
    up_b = lax.rem(me_b + 1, BRICKS)
    dn_b = lax.rem(me_b + BRICKS - 1, BRICKS)
    up_g = lax.rem(me_g + 1, GROUPS)
    dn_g = lax.rem(me_g + GROUPS - 1, GROUPS)
    is_mid = (me_g == MIDDLE) | (me_g == MIDDLE + 1)
    mid = jnp.where(me_g == MIDDLE, 0, 1)
    peers = [(lax.rem(me_g + k, GROUPS), me_b) for k in range(1, GROUPS)]
    beside = [(me_g, up_b), (me_g, dn_b)]
    even = lax.rem(me_b, 2) == 0
    pair = [(me_g, jnp.where(even, up_b, dn_b)), (me_g, jnp.where(even, dn_b, up_b))]
    side = jnp.where(even, 1.0, -1.0)
    corners = [(up_g, up_b), (up_g, dn_b), (dn_g, up_b), (dn_g, dn_b)]

    far_mids = [(MIDDLE, pair[1][1]), (MIDDLE + 1, pair[1][1])]

    barrier = pltpu.get_barrier_semaphore()
    pl.semaphore_signal(barrier, inc=1, device_id=pair[1], device_id_type=MESH)

    loads = {}
    for n, (name, source, target) in enumerate(
        (
            ("pos", pos_hbm, pos_in),
            ("vel", vel_hbm, vel_in),
            ("kick", kick_hbm, kick_in),
            ("type", type_hbm, type_in),
            ("count", count_hbm, count_in),
            ("pop", pop_hbm, pop_in),
            ("rows", rows_hbm, rows_in),
            ("partner", partner_hbm, partner_in),
        )
    ):
        loads[name] = pltpu.make_async_copy(source, target, sem_in.at[n])
        loads[name].start()

    partners = pair[::-1] + [peers[k - 1] for k in FARTHEST] + corners
    for device in partners[1:]:
        pl.semaphore_signal(barrier, inc=1, device_id=device, device_id_type=MESH)

    unsent = []

    def remote(src, dst, send_sem, recv_sem, device):
        return pltpu.make_async_remote_copy(
            src_ref=src,
            dst_ref=dst,
            send_sem=send_sem,
            recv_sem=recv_sem,
            device_id=device,
            device_id_type=MESH,
        )

    def send(*args):
        copy = remote(*args)
        copy.start()
        unsent.append(copy)
        return copy

    for name in ("pos", "vel", "kick", "type", "count"):
        loads[name].wait()
    slot_ids = lax.broadcasted_iota(jnp.int32, (CAP, NZ), 0)
    count = count_in[...]
    occupied = slot_ids < count
    tails = type_in[...].astype(F32)
    own_tail = type_in[...] == 1
    for c in range(2):
        half = slice(8 * c, 8 * c + 8)
        cur[0, c, 0] = jnp.where(occupied[half], pos_in[0, half], FAR)
        for axis in range(1, 3):
            cur[0, c, axis] = pos_in[axis, half]
        for axis in range(3):
            cur[0, c, 3 + axis] = vel_in[axis, half]
        cur[0, c, 6] = kick_in[0, half]
        cur[0, c, 7] = tails[half]

    pl.semaphore_wait(barrier, len(partners))

    @pl.when(is_mid)
    def _():
        pl.semaphore_signal(sem_entered, inc=1, device_id=pair[1], device_id_type=MESH)

    def send_near(source, target, sems):
        return send(source, target, sems.at[0, 0], sems.at[1, 0], pair[0])

    def send_far(source, target, sems, c):
        return send(source, target, sems.at[0, 1 + c], sems.at[1, 1 + c], pair[1])

    far_copies = [send_far(cur.at[0, c], cur.at[2, c], sem_cur, c) for c in range(2)]
    near_copy = send_near(cur.at[0], cur.at[1], sem_cur)
    cur_copies = far_copies + [near_copy]

    row_ids = me_g * LY + lax.broadcasted_iota(jnp.int32, (LY, NZ), 0)
    first_row = lax.broadcasted_iota(jnp.int32, (LY, NZ), 0) == 0
    last_row = lax.broadcasted_iota(jnp.int32, (LY, NZ), 0) == LY - 1
    low_wall = first_row & (me_g == 0)
    high_wall = last_row & (me_g == GROUPS - 1)

    for name in ("pop", "rows"):
        loads[name].wait()
    at_cell = row_ids == rows_in[...]
    g = [pop_in[q] for q in range(Q)]
    density, inverse, velocity = moments(g)

    def drag_copies():
        return [
            remote(drag.at[mid], drag.at[mid], sem_drag.at[k - 1], sem_drag.at[16 + mid], peers[k - 1])
            for k in FARTHEST
        ]

    @pl.when(is_mid)
    def _():
        for axis in range(3):
            drag[mid, axis : axis + 1, :] = jnp.sum(
                jnp.where(at_cell, velocity[axis], 0.0), axis=0, keepdims=True
            )
        for copy in drag_copies():
            copy.start()

    kick_copies = [
        send(kick_in.at[pl.ds(1, 2)], halo_kick.at[way], sem_kick.at[0, way], sem_kick.at[1, way], pair[way])
        for way in range(2)
    ]

    def store_post(stage, values):
        for q in range(Q):
            post[stage, q] = values[q]
        for way in range(2):
            for n, q in enumerate(TO_BRICK[way]):
                x_send[stage, way, n] = values[q]
            edge = LY - 1 if way == 0 else 0
            for n, q in enumerate(TO_GROUP[way]):
                row_send[stage, way, n] = values[q][edge : edge + 1, :]

    store_post(0, collide(g, density, inverse, velocity))

    def send_post(stage):
        copies = []
        for way in range(2):
            copies.append(
                send(
                    x_send.at[stage, way],
                    x_halo.at[stage, way],
                    sem_x.at[0, stage, way],
                    sem_x.at[1, stage, way],
                    beside[way],
                )
            )
        for way in range(2):
            group = (up_g, dn_g)[way]
            for n, (start, size, brick) in enumerate(((0, 3, me_b), (3, 1, up_b), (4, 1, dn_b))):
                copies.append(
                    send(
                        row_send.at[stage, way, pl.ds(start, size)],
                        row_halo.at[stage, way, pl.ds(start, size)],
                        sem_row.at[0, stage, way, n],
                        sem_row.at[1, stage, way, n],
                        (group, brick),
                    )
                )
        return copies

    def stream(stage):
        moved = []
        for q in range(Q):
            cx, cy, cz = VELOCITY_SET[q]
            if cx == 0:
                value = post[stage, q]
            else:
                way = 0 if cx > 0 else 1
                value = x_halo[stage, way, TO_BRICK[way].index(q)]
            if cy:
                way = 0 if cy > 0 else 1
                edge = row_halo[stage, way, TO_GROUP[way].index(q)]
                value = pltpu.roll(value, 1 if cy > 0 else LY - 1, 0)
                value = jnp.where(first_row if cy > 0 else last_row, edge, value)
            if cz:
                value = pltpu.roll(value, 1 if cz > 0 else NZ - 1, 1)
            if cy:
                value = jnp.where(
                    low_wall if cy > 0 else high_wall, post[stage, OPPOSITE[q]], value
                )
            moved.append(value)
        return moved

    post_copies = send_post(0)

    def load_near(step, k, c):
        half = slice(8 * c, 8 * c + 8)
        shift = (0.0, side, -side)[k]
        places = [cur[k, c, axis] for axis in range(3)]
        if k == 0 or step == 0:
            speeds = [cur[k, c, 3 + axis] for axis in range(3)]
        else:
            speeds = [halo_vel[step - 1, k - 1, c, axis] for axis in range(3)]
            places = [p + TIME_STEP * v for p, v in zip(places, speeds)]
            if step < STEPS - 1:
                for axis in range(3):
                    cur[k, c, axis] = places[axis]
        if step == 0:
            kick = cur[k, c, 6]
        elif k == 0:
            kick = kick_in[step, half]
        else:
            kick = halo_kick[k - 1, step - 1, half]
        tail = cur[k, c, 7]
        push = KICK_SCALE * kick
        fields = [
            places[0] + shift,
            places[1],
            places[2],
            FRICTION * speeds[0],
            FRICTION * speeds[1],
            FRICTION * speeds[2],
            push + (REPEL_SAME + (REPEL_CROSS - REPEL_SAME) * tail),
            push + (REPEL_CROSS + (REPEL_SAME - REPEL_CROSS) * tail),
        ]
        for n, b in enumerate((-1, 0, 1)):
            for f, field in enumerate(fields):
                if b:
                    field = pltpu.roll(field, (-b) % NZ, 1)
                if f == 2:
                    field = field + float(b)
                near[c, n, f] = field

    def add_forces(step, c, own, totals):
        half = slice(8 * own, 8 * own + 8)
        xi, yi, zi = [cur[0, own, axis] for axis in range(3)]
        ui, vi, wi = [FRICTION * cur[0, own, 3 + axis] for axis in range(3)]
        ki = KICK_SCALE * kick_in[step, half]
        tail = own_tail[half]
        fx, fy, fz = totals
        for n in range(3):
            for j in range(8):
                xj, yj, zj, uj, vj, wj, a0, a1 = [near[c, n, f, j : j + 1, :] for f in range(8)]
                dx = xi - xj
                dy = yi - yj
                dz = zi - zj
                weight = jnp.maximum(1.0 - (dx * dx + dy * dy + dz * dz), 0.0)
                closing = dx * (ui - uj) + dy * (vi - vj) + dz * (wi - wj)
                lift = jnp.where(tail, a1, a0) + ki
                strength = weight * (lift - weight * closing)
                fx = fx + strength * dx
                fy = fy + strength * dy
                fz = fz + strength * dz
        return fx, fy, fz

    loads["partner"].wait()
    partner = partner_in[...]
    partner = jnp.where(partner < count, partner, slot_ids)

    def bond_forces(own):
        places = [cur[0, own, axis] for axis in range(3)]
        found = list(places)
        for j in range(CAP):
            match = partner[8 * own : 8 * own + 8] == j
            for axis in range(3):
                found[axis] = jnp.where(match, cur[0, j // 8, axis, j % 8 : j % 8 + 1, :], found[axis])
        return tuple(-BOND_STIFF * (p - f) for p, f in zip(places, found))

    def cell_copies():
        other = MIDDLE + 1 - mid
        targets = [(other, me_b, 0), (me_g, up_b, 2), (other, up_b, 2)]
        targets += [(me_g, dn_b, 1), (other, dn_b, 1)]
        copies = []
        for n, (group, brick, column) in enumerate(targets):
            copies.append(
                remote(
                    cells.at[0, mid],
                    cells.at[column, mid],
                    sem_cell.at[n],
                    sem_cell.at[5 + 2 * column + mid],
                    (group, brick),
                )
            )
        return copies

    def lattice_between():
        for copy in post_copies:
            copy.wait_recv()
        g = stream(0)
        density, inverse, velocity = moments(g)
        store_post(1, collide(g, density, inverse, velocity))
        copies = send_post(1)

        @pl.when(is_mid)
        def _():
            pl.semaphore_wait(sem_entered, 1)
            for n in range(GROUPS):
                pl.semaphore_signal(
                    sem_ready, inc=1, device_id=(n, pair[1][1]), device_id_type=MESH
                )
            for n, value in enumerate([density] + velocity + [row_ids.astype(F32)]):
                cells[0, mid, n : n + 1, :] = jnp.sum(
                    jnp.where(at_cell, value, 0.0), axis=0, keepdims=True
                )
            for copy in cell_copies():
                copy.start()

        return copies

    def advance(step, own, totals):
        half = slice(8 * own, 8 * own + 8)
        for axis in range(3):
            speed = cur[0, own, 3 + axis]
            force = totals[axis] + (flow[axis : axis + 1] - DRAG_RATE * speed)
            speed = jnp.where(occupied[half], speed + TIME_STEP * force, 0.0)
            cur[0, own, 3 + axis] = speed
            if step < STEPS - 1:
                vel_send[step, own, axis] = speed
            else:
                vel_out[axis, half] = speed

    for step in range(STEPS):
        totals = [bond_forces(own) for own in range(2)]
        for k in range(3):
            if step == 1 and k == 2:
                post_copies = lattice_between()
            if k == 1:
                near_copy.wait_recv()
            if step == 1 and k:
                kick_copies[k - 1].wait_recv()
            for c in range(2):
                if k == 2:
                    far_copies[c].wait_recv()
                load_near(step, k, c)
                if step == 0 and k == 2 and c == 1:
                    for n in range(2):

                        @pl.when(me_g != MIDDLE + n)
                        def _():
                            remote(
                                drag.at[n], drag.at[n], sem_drag.at[0], sem_drag.at[16 + n], peers[0]
                            ).wait_recv()

                    flow = (DRAG_RATE / VELOCITY_SCALE) * (drag[0, 0:3] + drag[1, 0:3])
                    for copy in cur_copies:
                        copy.wait_send()
                sent = []
                for own in range(2):
                    totals[own] = add_forces(step, c, own, totals[own])
                    if k == 2 and c == 1:
                        advance(step, own, totals[own])
                        if step < STEPS - 1:
                            sent.append(
                                send_far(
                                    vel_send.at[step, own],
                                    halo_vel.at[step, 1, own],
                                    sem_vel.at[step],
                                    own,
                                )
                            )
        if step < STEPS - 1:
            far_copies = sent
            near_copy = send_near(vel_send.at[step], halo_vel.at[step, 0], sem_vel.at[step])
            for own in range(2):
                for axis in range(3):
                    cur[0, own, axis] += TIME_STEP * cur[0, own, 3 + axis]

    for axis in range(3):
        sums[me_g, axis : axis + 1, :] = jnp.sum(
            cur[0, 0, 3 + axis] + cur[0, 1, 3 + axis], axis=0, keepdims=True
        )
    sums[me_g, 3:4, :] = count.astype(F32)
    for k in FARTHEST:
        remote(sums.at[me_g], sums.at[me_g], sem_sum.at[0], sem_sum.at[1], peers[k - 1]).start()
    pl.semaphore_wait(sem_ready, len(far_mids))
    for n in range(2):
        remote(
            sums.at[me_g], sums.at[GROUPS + me_g], sem_sum.at[0], sem_sum.at[2], far_mids[n]
        ).start()

    def all_sums(start, size, recv_sem):
        part = sums.at[pl.ds(start, size)]
        return remote(part, part, sem_sum.at[0], recv_sem, peers[0])

    for axis in range(3):
        for own in range(2):
            half = slice(8 * own, 8 * own + 8)
            place = cur[0, own, axis] + TIME_STEP * cur[0, own, 3 + axis]
            pos_out[axis, half] = jnp.where(occupied[half], place, 0.0)
    for copy in post_copies:
        copy.wait_recv()
    g = stream(1)
    for q in range(Q):
        pop_out[q] = g[q]

    for copy in unsent:
        if not any(copy is other for other in cur_copies):
            copy.wait_send()

    def pooled(which):
        total = sums[GROUPS * which]
        for n in range(1, GROUPS):
            total = total + sums[GROUPS * which + n]
        return total[0:3] / total[3:4]

    all_sums(0, GROUPS - 1, sem_sum.at[1]).wait_recv()
    mean = pooled(0)
    for axis in range(3):
        mean_out[axis] = mean[axis : axis + 1]

    @pl.when(is_mid)
    def _():
        means[2, 0:3] = mean
        mean_copy = remote(means.at[2], means.at[0], sem_mean.at[0], sem_mean.at[1], pair[0])
        mean_copy.start()
        for column in range(3):
            for n in range(2):
                wait = remote(
                    cells.at[0, mid],
                    cells.at[column, n],
                    sem_cell.at[0],
                    sem_cell.at[5 + 2 * column + n],
                    beside[0],
                )
                if column:
                    wait.wait_recv()
                else:

                    @pl.when(mid != n)
                    def _():
                        wait.wait_recv()

        def change(column, column_mean, members):
            cell = cells[column, 0] + cells[column, 1]
            density = cell[0:1]
            inverse = 1.0 / density
            row = cell[4:5].astype(jnp.int32)
            before, after = [], []
            for axis in range(3):
                speed = cell[1 + axis : 2 + axis]
                force = VELOCITY_SCALE * column_mean[axis : axis + 1] - speed
                pushed = speed + (RELAX_TIME * PUSH) * inverse if axis == 0 else speed
                before.append(pushed)
                after.append(pushed + RELAX_TIME * force * inverse)
            square = sum(a * a - b * b for a, b in zip(after, before))
            for q in members:
                cx, cy, cz = VELOCITY_SET[q]
                change = -1.5 * square
                if q:
                    a, b = along(q, after), along(q, before)
                    change = change + (a - b) * (3.0 + 4.5 * (a + b))
                change = (1.0 / RELAX_TIME) * density * change
                tile = jnp.where(row_ids == row + cy, change, 0.0)
                if cz:
                    tile = pltpu.roll(tile, 1 if cz > 0 else NZ - 1, 1)
                pop_out[q] += tile

        change(0, mean, [q for q in range(Q) if VELOCITY_SET[q][0] == 0])
        mean_copy.wait_recv()
        all_sums(GROUPS, GROUPS, sem_sum.at[2]).wait_recv()
        far_mean = pooled(1)
        near_mean = means[0, 0:3]
        change(1, jnp.where(even, near_mean, far_mean), TO_BRICK[1])
        change(2, jnp.where(even, far_mean, near_mean), TO_BRICK[0])
        mean_copy.wait_send()
        for copy in cell_copies():
            copy.wait_send()
        for copy in drag_copies():
            copy.wait_send()

    all_sums(0, GROUPS + 1, sem_sum.at[1]).wait_send()


def hand_out(*refs):
    sources, targets, sem = refs[:4], refs[4:8], refs[8]
    copies = [
        pltpu.make_async_copy(source, target, sem.at[n])
        for n, (source, target) in enumerate(zip(sources, targets))
    ]
    for copy in copies:
        copy.start()
    for copy in copies:
        copy.wait()


def local(
    populations, membrane_rows, positions, velocities, kicks, bead_types, bond_partner, tile_counts
):
    vmem = pl.BlockSpec(memory_space=pltpu.VMEM)
    hbm = pl.BlockSpec(memory_space=pltpu.HBM)
    anywhere = pl.BlockSpec(memory_space=pl.ANY)
    dma = pltpu.SemaphoreType.DMA
    bead = (CAP, NZ)
    outs = pl.pallas_call(
        kernel,
        out_shape=(
            pltpu.VMEM((Q, LY, NZ), F32),
            pltpu.VMEM((3, 1, NZ), F32),
            pltpu.VMEM((3, *bead), F32),
            pltpu.VMEM((3, *bead), F32),
        ),
        in_specs=[hbm] * 8,
        out_specs=[vmem] * 4,
        scratch_shapes=[
            pltpu.VMEM((Q, LY, NZ), F32),
            pltpu.VMEM((1, NZ), jnp.int32),
            pltpu.VMEM((3, *bead), F32),
            pltpu.VMEM((3, *bead), F32),
            pltpu.VMEM((STEPS, *bead), F32),
            pltpu.VMEM(bead, jnp.int32),
            pltpu.VMEM(bead, jnp.int32),
            pltpu.VMEM((1, NZ), jnp.int32),
            dma((8,)),
            pltpu.VMEM((3, 2, 8, 8, NZ), F32),
            pltpu.VMEM((2, 2, *bead), F32),
            pltpu.VMEM((2, 2, 3, 8, NZ), F32),
            pltpu.VMEM((2, 2, 2, 3, 8, NZ), F32),
            pltpu.VMEM((2, 3, 8, 8, NZ), F32),
            pltpu.VMEM((2, 4, NZ), F32),
            pltpu.VMEM((2, Q, LY, NZ), F32),
            pltpu.VMEM((2, 2, 5, LY, NZ), F32),
            pltpu.VMEM((2, 2, 5, LY, NZ), F32),
            pltpu.VMEM((2, 2, 5, 1, NZ), F32),
            pltpu.VMEM((2, 2, 5, 1, NZ), F32),
            pltpu.VMEM((3, 2, 8, NZ), F32),
            pltpu.VMEM((2 * GROUPS, 4, NZ), F32),
            pltpu.VMEM((3, 8, NZ), F32),
            dma((2, 3)),
            dma((2, 2)),
            dma((2, 2, 3)),
            dma((18,)),
            dma((2, 2, 2)),
            dma((2, 2, 2, 3)),
            dma((11,)),
            dma((3,)),
            dma((2,)),
            pltpu.SemaphoreType.REGULAR,
            pltpu.SemaphoreType.REGULAR,
        ],
        compiler_params=pltpu.CompilerParams(
            collective_id=0, has_side_effects=True, vmem_limit_bytes=4 << 20
        ),
        name="cycle",
    )(
        *(
            pltpu.with_memory_space_constraint(x, pltpu.HBM)
            for x in (
                populations.reshape(Q, LY, NZ),
                membrane_rows,
                positions.reshape(3, *bead),
                velocities.reshape(3, *bead),
                kicks.reshape(STEPS, *bead),
                bead_types.reshape(bead),
                bond_partner.reshape(bead),
                tile_counts.reshape(1, NZ),
            )
        )
    )
    second, mean, places, speeds = pl.pallas_call(
        hand_out,
        out_shape=tuple(jax.ShapeDtypeStruct(x.shape, F32) for x in outs),
        in_specs=[anywhere] * 4,
        out_specs=[hbm] * 4,
        scratch_shapes=[dma((4,))],
        compiler_params=pltpu.CompilerParams(vmem_limit_bytes=1 << 20),
        name="hand_out",
    )(*outs)
    return (
        second.reshape(Q, 1, LY, NZ),
        mean,
        places.reshape(1, 3, CAP, 1, NZ),
        speeds.reshape(1, 3, CAP, 1, NZ),
    )


def solution(mesh):
    return jax.shard_map(
        local,
        mesh=mesh,
        in_specs=(
            P(None, "brick", "group", None),
            P("brick", None),
            P("group", None, None, "brick", None),
            P("group", None, None, "brick", None),
            P("group", None, None, "brick", None),
            P("group", None, "brick", None),
            P("group", None, "brick", None),
            P("group", "brick", None),
        ),
        out_specs=(
            P(None, "brick", "group", None),
            P(None, "brick", None),
            P("group", None, None, "brick", None),
            P("group", None, None, "brick", None),
        ),
        check_vma=False,
    )
```

```python
import math

import jax
import jax.numpy as jnp
import numpy as np
from jax import lax
from jax.experimental import pallas as pl
from jax.experimental.pallas import tpu as pltpu
from jax.sharding import PartitionSpec as P

VELOCITY_SET = (
    (0, 0, 0),
    (1, 0, 0),
    (-1, 0, 0),
    (0, 1, 0),
    (0, -1, 0),
    (0, 0, 1),
    (0, 0, -1),
    (1, 1, 0),
    (-1, -1, 0),
    (1, -1, 0),
    (-1, 1, 0),
    (1, 0, 1),
    (-1, 0, -1),
    (1, 0, -1),
    (-1, 0, 1),
    (0, 1, 1),
    (0, -1, -1),
    (0, 1, -1),
    (0, -1, 1),
)
WEIGHT_SET = (1.0 / 3.0,) + (1.0 / 18.0,) * 6 + (1.0 / 36.0,) * 12
OPPOSITE = (0, 2, 1, 4, 3, 6, 5, 8, 7, 10, 9, 12, 11, 14, 13, 16, 15, 18, 17)
Q = 19
TO_BRICK = ((1, 7, 9, 11, 13), (2, 8, 10, 12, 14))
TO_GROUP = ((3, 15, 17, 7, 10), (4, 16, 18, 9, 8))
RELAX_TIME = 0.8
PUSH = 0.001
VELOCITY_SCALE = 0.1
DRAG_RATE = 5.0
REPEL_SAME = 25.0
REPEL_CROSS = 50.0
FRICTION = 4.5
KICK_SCALE = 3.0 / math.sqrt(0.02) / math.sqrt(2.0)
TIME_STEP = 0.02
BOND_STIFF = 10.0
FAR = 1.0e8

GROUPS, BRICKS = 16, 32
CAP, NZ, LY, STEPS = 16, 128, 8, 3
MIDDLE = 7
FARTHEST = (8, 7, 9, 6, 10, 5, 11, 4, 12, 3, 13, 2, 14, 1, 15)
MESH = pl.DeviceIdType.MESH
F32 = jnp.float32


def moments(g):
    def total(signs):
        parts = []
        for weight, members in ((1.0 / 18.0, range(1, 7)), (1.0 / 36.0, range(7, 19))):
            part = None
            for q in members:
                if signs[q]:
                    if part is None:
                        part = g[q] if signs[q] > 0 else -g[q]
                    else:
                        part = part + g[q] if signs[q] > 0 else part - g[q]
            parts.append(part * weight)
        return parts[0] + parts[1]

    density = g[0] * (1.0 / 3.0) + total((1,) * Q)
    inverse = 1.0 / density
    velocity = [total([c[axis] for c in VELOCITY_SET]) * inverse for axis in range(3)]
    return density, inverse, velocity


def along(q, s):
    value = None
    for axis in range(3):
        sign = VELOCITY_SET[q][axis]
        if sign:
            if value is None:
                value = s[axis] if sign > 0 else -s[axis]
            else:
                value = value + s[axis] if sign > 0 else value - s[axis]
    return value


def collide(g, density, inverse, velocity):
    s = [velocity[0] + (RELAX_TIME * PUSH) * inverse, velocity[1], velocity[2]]
    rest = 1.0 - 1.5 * (s[0] * s[0] + s[1] * s[1] + s[2] * s[2])
    post = []
    for q in range(Q):
        if q == 0:
            equilibrium = density * rest
        else:
            a = along(q, s)
            equilibrium = density * (rest + a * (3.0 + 4.5 * a))
        post.append(g[q] - (g[q] - equilibrium) * (1.0 / RELAX_TIME))
    return post


def kernel(
    pop_hbm,
    rows_hbm,
    pos_hbm,
    vel_hbm,
    kick_hbm,
    type_hbm,
    partner_hbm,
    count_hbm,
    pop_out,
    mean_out,
    pos_out,
    vel_out,
    pop_in,
    rows_in,
    pos_in,
    vel_in,
    kick_in,
    type_in,
    partner_in,
    count_in,
    sem_in,
    cur,
    halo_kick,
    vel_send,
    halo_vel,
    near,
    drag,
    post,
    x_send,
    x_halo,
    row_send,
    row_halo,
    cells,
    sums,
    means,
    sem_cur,
    sem_kick,
    sem_vel,
    sem_drag,
    sem_x,
    sem_row,
    sem_cell,
    sem_sum,
    sem_mean,
    sem_entered,
    sem_ready,
    sem_corner,
):
    me_g = lax.axis_index("group")
    me_b = lax.axis_index("brick")
    up_b = lax.rem(me_b + 1, BRICKS)
    dn_b = lax.rem(me_b + BRICKS - 1, BRICKS)
    up_g = lax.rem(me_g + 1, GROUPS)
    dn_g = lax.rem(me_g + GROUPS - 1, GROUPS)
    is_mid = (me_g == MIDDLE) | (me_g == MIDDLE + 1)
    mid = jnp.where(me_g == MIDDLE, 0, 1)
    peers = [(lax.rem(me_g + k, GROUPS), me_b) for k in range(1, GROUPS)]
    beside = [(me_g, up_b), (me_g, dn_b)]
    even = lax.rem(me_b, 2) == 0
    pair = [(me_g, jnp.where(even, up_b, dn_b)), (me_g, jnp.where(even, dn_b, up_b))]
    side = jnp.where(even, 1.0, -1.0)

    far_mids = [(MIDDLE, pair[1][1]), (MIDDLE + 1, pair[1][1])]

    barrier = pltpu.get_barrier_semaphore()
    pl.semaphore_signal(barrier, inc=1, device_id=pair[1], device_id_type=MESH)

    loads = {}
    for n, (name, source, target) in enumerate(
        (
            ("pos", pos_hbm, pos_in),
            ("vel", vel_hbm, vel_in),
            ("kick", kick_hbm, kick_in),
            ("type", type_hbm, type_in),
            ("count", count_hbm, count_in),
            ("pop", pop_hbm, pop_in),
            ("rows", rows_hbm, rows_in),
            ("partner", partner_hbm, partner_in),
        )
    ):
        loads[name] = pltpu.make_async_copy(source, target, sem_in.at[n])
        loads[name].start()

    pl.semaphore_signal(barrier, inc=1, device_id=pair[0], device_id_type=MESH)
    for n in range(2):

        @pl.when(me_g != MIDDLE + n)
        def _():
            pl.semaphore_signal(
                barrier, inc=1, device_id=(MIDDLE + n, me_b), device_id_type=MESH
            )

    for group in (up_g, dn_g):
        pl.semaphore_signal(barrier, inc=1, device_id=(group, me_b), device_id_type=MESH)

    unsent = []

    def remote(src, dst, send_sem, recv_sem, device):
        return pltpu.make_async_remote_copy(
            src_ref=src,
            dst_ref=dst,
            send_sem=send_sem,
            recv_sem=recv_sem,
            device_id=device,
            device_id_type=MESH,
        )

    def send(*args):
        copy = remote(*args)
        copy.start()
        unsent.append(copy)
        return copy

    for name in ("pos", "vel", "kick", "type", "count"):
        loads[name].wait()
    slot_ids = lax.broadcasted_iota(jnp.int32, (CAP, NZ), 0)
    count = count_in[...]
    occupied = slot_ids < count
    tails = type_in[...].astype(F32)
    own_tail = type_in[...] == 1
    for c in range(2):
        half = slice(8 * c, 8 * c + 8)
        cur[0, c, 0] = jnp.where(occupied[half], pos_in[0, half], FAR)
        for axis in range(1, 3):
            cur[0, c, axis] = pos_in[axis, half]
        for axis in range(3):
            cur[0, c, 3 + axis] = vel_in[axis, half]
        cur[0, c, 6] = kick_in[0, half]
        cur[0, c, 7] = tails[half]

    pl.semaphore_wait(barrier, jnp.where(is_mid, 4 + GROUPS - 1, 4))

    def send_near(source, target, sems):
        return send(source, target, sems.at[0, 0], sems.at[1, 0], pair[0])

    def send_far(source, target, sems, c):
        return send(source, target, sems.at[0, 1 + c], sems.at[1, 1 + c], pair[1])

    far_copies = [send_far(cur.at[0, c], cur.at[2, c], sem_cur, c) for c in range(2)]
    near_copy = send_near(cur.at[0], cur.at[1], sem_cur)
    cur_copies = far_copies + [near_copy]

    for group in (up_g, dn_g):
        pl.semaphore_signal(sem_corner, inc=1, device_id=(group, me_b), device_id_type=MESH)

    @pl.when(is_mid)
    def _():
        pl.semaphore_signal(sem_entered, inc=1, device_id=pair[1], device_id_type=MESH)

    row_ids = me_g * LY + lax.broadcasted_iota(jnp.int32, (LY, NZ), 0)
    first_row = lax.broadcasted_iota(jnp.int32, (LY, NZ), 0) == 0
    last_row = lax.broadcasted_iota(jnp.int32, (LY, NZ), 0) == LY - 1
    low_wall = first_row & (me_g == 0)
    high_wall = last_row & (me_g == GROUPS - 1)

    for name in ("pop", "rows"):
        loads[name].wait()
    at_cell = row_ids == rows_in[...]
    g = [pop_in[q] for q in range(Q)]
    density, inverse, velocity = moments(g)

    def drag_copies():
        return [
            remote(drag.at[mid], drag.at[mid], sem_drag.at[k - 1], sem_drag.at[16 + mid], peers[k - 1])
            for k in FARTHEST
        ]

    @pl.when(is_mid)
    def _():
        for axis in range(3):
            drag[mid, axis : axis + 1, :] = jnp.sum(
                jnp.where(at_cell, velocity[axis], 0.0), axis=0, keepdims=True
            )
        for copy in drag_copies():
            copy.start()

    kick_copies = [
        send(kick_in.at[pl.ds(1, 2)], halo_kick.at[way], sem_kick.at[0, way], sem_kick.at[1, way], pair[way])
        for way in range(2)
    ]

    def store_post(stage, values):
        for q in range(Q):
            post[stage, q] = values[q]
        for way in range(2):
            for n, q in enumerate(TO_BRICK[way]):
                x_send[stage, way, n] = values[q]
            edge = LY - 1 if way == 0 else 0
            for n, q in enumerate(TO_GROUP[way]):
                row_send[stage, way, n] = values[q][edge : edge + 1, :]

    store_post(0, collide(g, density, inverse, velocity))

    def send_post(stage):
        copies = []
        for way in range(2):
            copies.append(
                send(
                    x_send.at[stage, way],
                    x_halo.at[stage, way],
                    sem_x.at[0, stage, way],
                    sem_x.at[1, stage, way],
                    beside[way],
                )
            )
        for way in range(2):
            group = (up_g, dn_g)[way]
            for n, (start, size, brick) in enumerate(((0, 3, me_b), (3, 1, up_b), (4, 1, dn_b))):
                copies.append(
                    send(
                        row_send.at[stage, way, pl.ds(start, size)],
                        row_halo.at[stage, way, pl.ds(start, size)],
                        sem_row.at[0, stage, way, n],
                        sem_row.at[1, stage, way, n],
                        (group, brick),
                    )
                )
        return copies

    def stream(stage):
        moved = []
        for q in range(Q):
            cx, cy, cz = VELOCITY_SET[q]
            if cx == 0:
                value = post[stage, q]
            else:
                way = 0 if cx > 0 else 1
                value = x_halo[stage, way, TO_BRICK[way].index(q)]
            if cy:
                way = 0 if cy > 0 else 1
                edge = row_halo[stage, way, TO_GROUP[way].index(q)]
                value = pltpu.roll(value, 1 if cy > 0 else LY - 1, 0)
                value = jnp.where(first_row if cy > 0 else last_row, edge, value)
            if cz:
                value = pltpu.roll(value, 1 if cz > 0 else NZ - 1, 1)
            if cy:
                value = jnp.where(
                    low_wall if cy > 0 else high_wall, post[stage, OPPOSITE[q]], value
                )
            moved.append(value)
        return moved

    def load_near(step, k, c):
        half = slice(8 * c, 8 * c + 8)
        shift = (0.0, side, -side)[k]
        places = [cur[k, c, axis] for axis in range(3)]
        if k == 0 or step == 0:
            speeds = [cur[k, c, 3 + axis] for axis in range(3)]
        else:
            speeds = [halo_vel[step - 1, k - 1, c, axis] for axis in range(3)]
            places = [p + TIME_STEP * v for p, v in zip(places, speeds)]
            if step < STEPS - 1:
                for axis in range(3):
                    cur[k, c, axis] = places[axis]
        if step == 0:
            kick = cur[k, c, 6]
        elif k == 0:
            kick = kick_in[step, half]
        else:
            kick = halo_kick[k - 1, step - 1, half]
        tail = cur[k, c, 7]
        push = KICK_SCALE * kick
        fields = [
            places[0] + shift,
            places[1],
            places[2],
            FRICTION * speeds[0],
            FRICTION * speeds[1],
            FRICTION * speeds[2],
            push + (REPEL_SAME + (REPEL_CROSS - REPEL_SAME) * tail),
            push + (REPEL_CROSS + (REPEL_SAME - REPEL_CROSS) * tail),
        ]
        for n, b in enumerate((-1, 0, 1)):
            for f, field in enumerate(fields):
                if b:
                    field = pltpu.roll(field, (-b) % NZ, 1)
                if f == 2:
                    field = field + float(b)
                near[c, n, f] = field

    def add_forces(step, c, own, totals):
        half = slice(8 * own, 8 * own + 8)
        xi, yi, zi = [cur[0, own, axis] for axis in range(3)]
        ui, vi, wi = [FRICTION * cur[0, own, 3 + axis] for axis in range(3)]
        ki = KICK_SCALE * kick_in[step, half]
        tail = own_tail[half]
        fx, fy, fz = totals
        for n in range(3):
            for j in range(8):
                xj, yj, zj, uj, vj, wj, a0, a1 = [near[c, n, f, j : j + 1, :] for f in range(8)]
                dx = xi - xj
                dy = yi - yj
                dz = zi - zj
                weight = jnp.maximum(1.0 - (dx * dx + dy * dy + dz * dz), 0.0)
                closing = dx * (ui - uj) + dy * (vi - vj) + dz * (wi - wj)
                lift = jnp.where(tail, a1, a0) + ki
                strength = weight * (lift - weight * closing)
                fx = fx + strength * dx
                fy = fy + strength * dy
                fz = fz + strength * dz
        return fx, fy, fz

    loads["partner"].wait()
    partner = partner_in[...]
    partner = jnp.where(partner < count, partner, slot_ids)

    def bond_forces(own):
        places = [cur[0, own, axis] for axis in range(3)]
        found = list(places)
        for j in range(CAP):
            match = partner[8 * own : 8 * own + 8] == j
            for axis in range(3):
                found[axis] = jnp.where(match, cur[0, j // 8, axis, j % 8 : j % 8 + 1, :], found[axis])
        return tuple(-BOND_STIFF * (p - f) for p, f in zip(places, found))

    def cell_copies():
        other = MIDDLE + 1 - mid
        targets = [(other, me_b, 0), (me_g, up_b, 2), (other, up_b, 2)]
        targets += [(me_g, dn_b, 1), (other, dn_b, 1)]
        copies = []
        for n, (group, brick, column) in enumerate(targets):
            copies.append(
                remote(
                    cells.at[0, mid],
                    cells.at[column, mid],
                    sem_cell.at[n],
                    sem_cell.at[5 + 2 * column + mid],
                    (group, brick),
                )
            )
        return copies

    def lattice_between():
        for copy in post_copies:
            copy.wait_recv()
        g = stream(0)
        density, inverse, velocity = moments(g)
        store_post(1, collide(g, density, inverse, velocity))
        copies = send_post(1)

        @pl.when(is_mid)
        def _():
            pl.semaphore_wait(sem_entered, 1)
            for n in range(GROUPS):
                pl.semaphore_signal(
                    sem_ready, inc=1, device_id=(n, pair[1][1]), device_id_type=MESH
                )
            for n, value in enumerate([density] + velocity + [row_ids.astype(F32)]):
                cells[0, mid, n : n + 1, :] = jnp.sum(
                    jnp.where(at_cell, value, 0.0), axis=0, keepdims=True
                )
            for copy in cell_copies():
                copy.start()

        return copies

    def advance(step, own, totals):
        half = slice(8 * own, 8 * own + 8)
        for axis in range(3):
            speed = cur[0, own, 3 + axis]
            force = totals[axis] + (flow[axis : axis + 1] - DRAG_RATE * speed)
            speed = jnp.where(occupied[half], speed + TIME_STEP * force, 0.0)
            cur[0, own, 3 + axis] = speed
            if step < STEPS - 1:
                vel_send[step, own, axis] = speed
            else:
                vel_out[axis, half] = speed

    def wait_drag():
        for n in range(2):

            @pl.when(me_g != MIDDLE + n)
            def _():
                remote(
                    drag.at[n], drag.at[n], sem_drag.at[0], sem_drag.at[16 + n], peers[0]
                ).wait_recv()

        for copy in cur_copies:
            copy.wait_send()
        return (DRAG_RATE / VELOCITY_SCALE) * (drag[0, 0:3] + drag[1, 0:3])

    for step in range(STEPS):
        totals = [bond_forces(own) for own in range(2)]
        for k in range(3):
            if step == 0 and k == 2:
                pl.semaphore_wait(sem_corner, 2)
                post_copies = send_post(0)
            if step == 1 and k == 2:
                post_copies = lattice_between()
            if k == 1:
                near_copy.wait_recv()
            if step == 1 and k:
                kick_copies[k - 1].wait_recv()
            for c in range(2):
                if k == 2:
                    far_copies[c].wait_recv()
                load_near(step, k, c)
                sent = []
                for own in range(2):
                    totals[own] = add_forces(step, c, own, totals[own])
                    if k == 2 and c == 1:
                        if step == 0 and own == 0:
                            flow = wait_drag()
                        advance(step, own, totals[own])
                        if step < STEPS - 1:
                            sent.append(
                                send_far(
                                    vel_send.at[step, own],
                                    halo_vel.at[step, 1, own],
                                    sem_vel.at[step],
                                    own,
                                )
                            )
        if step < STEPS - 1:
            far_copies = sent
            near_copy = send_near(vel_send.at[step], halo_vel.at[step, 0], sem_vel.at[step])
            for own in range(2):
                for axis in range(3):
                    cur[0, own, axis] += TIME_STEP * cur[0, own, 3 + axis]

    for axis in range(3):
        sums[me_g, axis : axis + 1, :] = jnp.sum(
            cur[0, 0, 3 + axis] + cur[0, 1, 3 + axis], axis=0, keepdims=True
        )
    sums[me_g, 3:4, :] = count.astype(F32)
    for k in FARTHEST:
        remote(sums.at[me_g], sums.at[me_g], sem_sum.at[0], sem_sum.at[1], peers[k - 1]).start()
    pl.semaphore_wait(sem_ready, len(far_mids))
    for n in range(2):
        remote(
            sums.at[me_g], sums.at[GROUPS + me_g], sem_sum.at[0], sem_sum.at[2], far_mids[n]
        ).start()

    def all_sums(start, size, recv_sem):
        part = sums.at[pl.ds(start, size)]
        return remote(part, part, sem_sum.at[0], recv_sem, peers[0])

    for axis in range(3):
        for own in range(2):
            half = slice(8 * own, 8 * own + 8)
            place = cur[0, own, axis] + TIME_STEP * cur[0, own, 3 + axis]
            pos_out[axis, half] = jnp.where(occupied[half], place, 0.0)
    for copy in post_copies:
        copy.wait_recv()
    g = stream(1)
    for q in range(Q):
        pop_out[q] = g[q]

    for copy in unsent:
        if not any(copy is other for other in cur_copies):
            copy.wait_send()

    def pooled(which):
        total = sums[GROUPS * which]
        for n in range(1, GROUPS):
            total = total + sums[GROUPS * which + n]
        return total[0:3] / total[3:4]

    all_sums(0, GROUPS - 1, sem_sum.at[1]).wait_recv()
    mean = pooled(0)
    for axis in range(3):
        mean_out[axis] = mean[axis : axis + 1]

    @pl.when(is_mid)
    def _():
        means[2, 0:3] = mean
        mean_copy = remote(means.at[2], means.at[0], sem_mean.at[0], sem_mean.at[1], pair[0])
        mean_copy.start()
        for column in range(3):
            for n in range(2):
                wait = remote(
                    cells.at[0, mid],
                    cells.at[column, n],
                    sem_cell.at[0],
                    sem_cell.at[5 + 2 * column + n],
                    beside[0],
                )
                if column:
                    wait.wait_recv()
                else:

                    @pl.when(mid != n)
                    def _():
                        wait.wait_recv()

        def change(column, column_mean, members):
            cell = cells[column, 0] + cells[column, 1]
            density = cell[0:1]
            inverse = 1.0 / density
            row = cell[4:5].astype(jnp.int32)
            before, after = [], []
            for axis in range(3):
                speed = cell[1 + axis : 2 + axis]
                force = VELOCITY_SCALE * column_mean[axis : axis + 1] - speed
                pushed = speed + (RELAX_TIME * PUSH) * inverse if axis == 0 else speed
                before.append(pushed)
                after.append(pushed + RELAX_TIME * force * inverse)
            square = sum(a * a - b * b for a, b in zip(after, before))
            for q in members:
                cx, cy, cz = VELOCITY_SET[q]
                change = -1.5 * square
                if q:
                    a, b = along(q, after), along(q, before)
                    change = change + (a - b) * (3.0 + 4.5 * (a + b))
                change = (1.0 / RELAX_TIME) * density * change
                tile = jnp.where(row_ids == row + cy, change, 0.0)
                if cz:
                    tile = pltpu.roll(tile, 1 if cz > 0 else NZ - 1, 1)
                pop_out[q] += tile

        change(0, mean, [q for q in range(Q) if VELOCITY_SET[q][0] == 0])
        mean_copy.wait_recv()
        all_sums(GROUPS, GROUPS, sem_sum.at[2]).wait_recv()
        far_mean = pooled(1)
        near_mean = means[0, 0:3]
        change(1, jnp.where(even, near_mean, far_mean), TO_BRICK[1])
        change(2, jnp.where(even, far_mean, near_mean), TO_BRICK[0])
        mean_copy.wait_send()
        for copy in cell_copies():
            copy.wait_send()
        for copy in drag_copies():
            copy.wait_send()

    all_sums(0, GROUPS + 1, sem_sum.at[1]).wait_send()


def hand_out(*refs):
    sources, targets, sem = refs[:4], refs[4:8], refs[8]
    copies = [
        pltpu.make_async_copy(source, target, sem.at[n])
        for n, (source, target) in enumerate(zip(sources, targets))
    ]
    for copy in copies:
        copy.start()
    for copy in copies:
        copy.wait()


def local(
    populations, membrane_rows, positions, velocities, kicks, bead_types, bond_partner, tile_counts
):
    vmem = pl.BlockSpec(memory_space=pltpu.VMEM)
    hbm = pl.BlockSpec(memory_space=pltpu.HBM)
    anywhere = pl.BlockSpec(memory_space=pl.ANY)
    dma = pltpu.SemaphoreType.DMA
    bead = (CAP, NZ)
    outs = pl.pallas_call(
        kernel,
        out_shape=(
            pltpu.VMEM((Q, LY, NZ), F32),
            pltpu.VMEM((3, 1, NZ), F32),
            pltpu.VMEM((3, *bead), F32),
            pltpu.VMEM((3, *bead), F32),
        ),
        in_specs=[hbm] * 8,
        out_specs=[vmem] * 4,
        scratch_shapes=[
            pltpu.VMEM((Q, LY, NZ), F32),
            pltpu.VMEM((1, NZ), jnp.int32),
            pltpu.VMEM((3, *bead), F32),
            pltpu.VMEM((3, *bead), F32),
            pltpu.VMEM((STEPS, *bead), F32),
            pltpu.VMEM(bead, jnp.int32),
            pltpu.VMEM(bead, jnp.int32),
            pltpu.VMEM((1, NZ), jnp.int32),
            dma((8,)),
            pltpu.VMEM((3, 2, 8, 8, NZ), F32),
            pltpu.VMEM((2, 2, *bead), F32),
            pltpu.VMEM((2, 2, 3, 8, NZ), F32),
            pltpu.VMEM((2, 2, 2, 3, 8, NZ), F32),
            pltpu.VMEM((2, 3, 8, 8, NZ), F32),
            pltpu.VMEM((2, 4, NZ), F32),
            pltpu.VMEM((2, Q, LY, NZ), F32),
            pltpu.VMEM((2, 2, 5, LY, NZ), F32),
            pltpu.VMEM((2, 2, 5, LY, NZ), F32),
            pltpu.VMEM((2, 2, 5, 1, NZ), F32),
            pltpu.VMEM((2, 2, 5, 1, NZ), F32),
            pltpu.VMEM((3, 2, 8, NZ), F32),
            pltpu.VMEM((2 * GROUPS, 4, NZ), F32),
            pltpu.VMEM((3, 8, NZ), F32),
            dma((2, 3)),
            dma((2, 2)),
            dma((2, 2, 3)),
            dma((18,)),
            dma((2, 2, 2)),
            dma((2, 2, 2, 3)),
            dma((11,)),
            dma((3,)),
            dma((2,)),
            pltpu.SemaphoreType.REGULAR,
            pltpu.SemaphoreType.REGULAR,
            pltpu.SemaphoreType.REGULAR,
        ],
        compiler_params=pltpu.CompilerParams(
            collective_id=0, has_side_effects=True, vmem_limit_bytes=4 << 20
        ),
        name="cycle",
    )(
        *(
            pltpu.with_memory_space_constraint(x, pltpu.HBM)
            for x in (
                populations.reshape(Q, LY, NZ),
                membrane_rows,
                positions.reshape(3, *bead),
                velocities.reshape(3, *bead),
                kicks.reshape(STEPS, *bead),
                bead_types.reshape(bead),
                bond_partner.reshape(bead),
                tile_counts.reshape(1, NZ),
            )
        )
    )
    second, mean, places, speeds = pl.pallas_call(
        hand_out,
        out_shape=tuple(jax.ShapeDtypeStruct(x.shape, F32) for x in outs),
        in_specs=[anywhere] * 4,
        out_specs=[hbm] * 4,
        scratch_shapes=[dma((4,))],
        compiler_params=pltpu.CompilerParams(vmem_limit_bytes=1 << 20),
        name="hand_out",
    )(*outs)
    return (
        second.reshape(Q, 1, LY, NZ),
        mean,
        places.reshape(1, 3, CAP, 1, NZ),
        speeds.reshape(1, 3, CAP, 1, NZ),
    )


def solution(mesh):
    return jax.shard_map(
        local,
        mesh=mesh,
        in_specs=(
            P(None, "brick", "group", None),
            P("brick", None),
            P("group", None, None, "brick", None),
            P("group", None, None, "brick", None),
            P("group", None, None, "brick", None),
            P("group", None, "brick", None),
            P("group", None, "brick", None),
            P("group", "brick", None),
        ),
        out_specs=(
            P(None, "brick", "group", None),
            P(None, "brick", None),
            P("group", None, None, "brick", None),
            P("group", None, None, "brick", None),
        ),
        check_vma=False,
    )
```

```python
import math

import jax
import jax.numpy as jnp
import numpy as np
from jax import lax
from jax.experimental import pallas as pl
from jax.experimental.pallas import tpu as pltpu
from jax.sharding import PartitionSpec as P

VELOCITY_SET = (
    (0, 0, 0),
    (1, 0, 0),
    (-1, 0, 0),
    (0, 1, 0),
    (0, -1, 0),
    (0, 0, 1),
    (0, 0, -1),
    (1, 1, 0),
    (-1, -1, 0),
    (1, -1, 0),
    (-1, 1, 0),
    (1, 0, 1),
    (-1, 0, -1),
    (1, 0, -1),
    (-1, 0, 1),
    (0, 1, 1),
    (0, -1, -1),
    (0, 1, -1),
    (0, -1, 1),
)
WEIGHT_SET = (1.0 / 3.0,) + (1.0 / 18.0,) * 6 + (1.0 / 36.0,) * 12
OPPOSITE = (0, 2, 1, 4, 3, 6, 5, 8, 7, 10, 9, 12, 11, 14, 13, 16, 15, 18, 17)
Q = 19
TO_BRICK = ((1, 7, 9, 11, 13), (2, 8, 10, 12, 14))
TO_GROUP = ((3, 15, 17, 7, 10), (4, 16, 18, 9, 8))
RELAX_TIME = 0.8
PUSH = 0.001
VELOCITY_SCALE = 0.1
DRAG_RATE = 5.0
REPEL_SAME = 25.0
REPEL_CROSS = 50.0
FRICTION = 4.5
KICK_SCALE = 3.0 / math.sqrt(0.02) / math.sqrt(2.0)
TIME_STEP = 0.02
BOND_STIFF = 10.0
FAR = 1.0e8

GROUPS, BRICKS = 16, 32
CAP, NZ, LY, STEPS = 16, 128, 8, 3
MIDDLE = 7
FARTHEST = (8, 7, 9, 6, 10, 5, 11, 4, 12, 3, 13, 2, 14, 1, 15)
MESH = pl.DeviceIdType.MESH
F32 = jnp.float32


def moments(g):
    def total(signs):
        parts = []
        for weight, members in ((1.0 / 18.0, range(1, 7)), (1.0 / 36.0, range(7, 19))):
            part = None
            for q in members:
                if signs[q]:
                    if part is None:
                        part = g[q] if signs[q] > 0 else -g[q]
                    else:
                        part = part + g[q] if signs[q] > 0 else part - g[q]
            parts.append(part * weight)
        return parts[0] + parts[1]

    density = g[0] * (1.0 / 3.0) + total((1,) * Q)
    inverse = 1.0 / density
    velocity = [total([c[axis] for c in VELOCITY_SET]) * inverse for axis in range(3)]
    return density, inverse, velocity


def along(q, s):
    value = None
    for axis in range(3):
        sign = VELOCITY_SET[q][axis]
        if sign:
            if value is None:
                value = s[axis] if sign > 0 else -s[axis]
            else:
                value = value + s[axis] if sign > 0 else value - s[axis]
    return value


def collide(g, density, inverse, velocity):
    s = [velocity[0] + (RELAX_TIME * PUSH) * inverse, velocity[1], velocity[2]]
    rest = 1.0 - 1.5 * (s[0] * s[0] + s[1] * s[1] + s[2] * s[2])
    post = []
    for q in range(Q):
        if q == 0:
            equilibrium = density * rest
        else:
            a = along(q, s)
            equilibrium = density * (rest + a * (3.0 + 4.5 * a))
        post.append(g[q] - (g[q] - equilibrium) * (1.0 / RELAX_TIME))
    return post


def kernel(
    pop_hbm,
    rows_hbm,
    pos_hbm,
    vel_hbm,
    kick_hbm,
    type_hbm,
    partner_hbm,
    count_hbm,
    pop_out,
    mean_out,
    pos_out,
    vel_out,
    pop_in,
    rows_in,
    pos_in,
    vel_in,
    kick_in,
    type_in,
    partner_in,
    count_in,
    sem_in,
    cur,
    partners,
    halo_kick,
    vel_send,
    halo_vel,
    near,
    drag,
    post,
    x_send,
    x_halo,
    row_send,
    row_halo,
    cells,
    sums,
    means,
    sem_cur,
    sem_partner,
    sem_kick,
    sem_vel,
    sem_drag,
    sem_x,
    sem_row,
    sem_cell,
    sem_sum,
    sem_mean,
    sem_corner,
):
    me_g = lax.axis_index("group")
    me_b = lax.axis_index("brick")
    up_b = lax.rem(me_b + 1, BRICKS)
    dn_b = lax.rem(me_b + BRICKS - 1, BRICKS)
    up_g = lax.rem(me_g + 1, GROUPS)
    dn_g = lax.rem(me_g + GROUPS - 1, GROUPS)
    is_mid = (me_g == MIDDLE) | (me_g == MIDDLE + 1)
    mid = jnp.where(me_g == MIDDLE, 0, 1)
    peers = [(lax.rem(me_g + k, GROUPS), me_b) for k in range(1, GROUPS)]
    beside = [(me_g, up_b), (me_g, dn_b)]
    even = lax.rem(me_b, 2) == 0
    pair = [(me_g, jnp.where(even, up_b, dn_b)), (me_g, jnp.where(even, dn_b, up_b))]
    side = jnp.where(even, 1.0, -1.0)
    ahead2 = (me_g, lax.rem(me_b + jnp.where(even, 2, BRICKS - 2), BRICKS))
    back2 = (me_g, lax.rem(me_b + jnp.where(even, BRICKS - 2, 2), BRICKS))
    targets = [pair[0], pair[1], ahead2]

    far_mids = [(MIDDLE, pair[1][1]), (MIDDLE + 1, pair[1][1])]

    barrier = pltpu.get_barrier_semaphore()
    pl.semaphore_signal(barrier, inc=1, device_id=pair[1], device_id_type=MESH)

    loads = {}
    for n, (name, source, target) in enumerate(
        (
            ("pos", pos_hbm, pos_in),
            ("vel", vel_hbm, vel_in),
            ("kick", kick_hbm, kick_in),
            ("type", type_hbm, type_in),
            ("count", count_hbm, count_in),
            ("pop", pop_hbm, pop_in),
            ("rows", rows_hbm, rows_in),
            ("partner", partner_hbm, partner_in),
        )
    ):
        loads[name] = pltpu.make_async_copy(source, target, sem_in.at[n])
        loads[name].start()

    for device in (pair[0], back2):
        pl.semaphore_signal(barrier, inc=1, device_id=device, device_id_type=MESH)
    for n in range(2):
        pl.semaphore_signal(barrier, inc=1, device_id=far_mids[n], device_id_type=MESH)

        @pl.when(me_g != MIDDLE + n)
        def _():
            pl.semaphore_signal(
                barrier, inc=1, device_id=(MIDDLE + n, me_b), device_id_type=MESH
            )

    for group in (up_g, dn_g):
        pl.semaphore_signal(barrier, inc=1, device_id=(group, me_b), device_id_type=MESH)

    unsent = []

    def remote(src, dst, send_sem, recv_sem, device):
        return pltpu.make_async_remote_copy(
            src_ref=src,
            dst_ref=dst,
            send_sem=send_sem,
            recv_sem=recv_sem,
            device_id=device,
            device_id_type=MESH,
        )

    def send(*args):
        copy = remote(*args)
        copy.start()
        unsent.append(copy)
        return copy

    for name in ("pos", "vel", "kick", "type", "count", "partner"):
        loads[name].wait()
    slot_ids = lax.broadcasted_iota(jnp.int32, (CAP, NZ), 0)
    count = count_in[...]
    occupied = slot_ids < count
    tails = type_in[...].astype(F32)
    partner = partner_in[...]
    partners[0] = jnp.where(partner < count, partner, slot_ids)
    for c in range(2):
        half = slice(8 * c, 8 * c + 8)
        cur[0, c, 0] = jnp.where(occupied[half], pos_in[0, half], FAR)
        for axis in range(1, 3):
            cur[0, c, axis] = pos_in[axis, half]
        for axis in range(3):
            cur[0, c, 3 + axis] = vel_in[axis, half]
        cur[0, c, 6] = kick_in[0, half]
        cur[0, c, 7] = tails[half]

    pl.semaphore_wait(barrier, jnp.where(is_mid, 5 + 2 * GROUPS - 1, 5))

    def spread(source, target, sems, which):
        return {
            k: send(source, target.at[k], sems.at[0, k - 1], sems.at[1, k - 1], targets[k - 1])
            for k in which
        }

    cur_copies = spread(cur.at[0], cur, sem_cur, (2, 3, 1))
    partner_copies = spread(partners.at[0], partners, sem_partner, (2,))

    for group in (up_g, dn_g):
        pl.semaphore_signal(sem_corner, inc=1, device_id=(group, me_b), device_id_type=MESH)

    row_ids = me_g * LY + lax.broadcasted_iota(jnp.int32, (LY, NZ), 0)
    first_row = lax.broadcasted_iota(jnp.int32, (LY, NZ), 0) == 0
    last_row = lax.broadcasted_iota(jnp.int32, (LY, NZ), 0) == LY - 1
    low_wall = first_row & (me_g == 0)
    high_wall = last_row & (me_g == GROUPS - 1)

    for name in ("pop", "rows"):
        loads[name].wait()
    at_cell = row_ids == rows_in[...]
    g = [pop_in[q] for q in range(Q)]
    density, inverse, velocity = moments(g)

    def drag_copies():
        copies = [
            remote(drag.at[0, mid], drag.at[0, mid], sem_drag.at[15 + k], sem_drag.at[31 + mid], peers[k - 1])
            for k in FARTHEST
        ]
        return copies + [
            remote(drag.at[0, mid], drag.at[1, mid], sem_drag.at[n], sem_drag.at[33 + mid], (n, pair[1][1]))
            for n in range(GROUPS)
        ]

    @pl.when(is_mid)
    def _():
        for axis in range(3):
            drag[0, mid, axis : axis + 1, :] = jnp.sum(
                jnp.where(at_cell, velocity[axis], 0.0), axis=0, keepdims=True
            )
        for copy in drag_copies():
            copy.start()

    kick_copies = spread(kick_in.at[pl.ds(1, 2)], halo_kick, sem_kick, (2, 1))
    kick_copies[3] = send(
        kick_in.at[1], halo_kick.at[3, 0], sem_kick.at[0, 2], sem_kick.at[1, 2], ahead2
    )

    def store_post(stage, values):
        for q in range(Q):
            post[stage, q] = values[q]
        for way in range(2):
            for n, q in enumerate(TO_BRICK[way]):
                x_send[stage, way, n] = values[q]
            edge = LY - 1 if way == 0 else 0
            for n, q in enumerate(TO_GROUP[way]):
                row_send[stage, way, n] = values[q][edge : edge + 1, :]

    store_post(0, collide(g, density, inverse, velocity))

    def send_post(stage):
        copies = []
        for way in range(2):
            copies.append(
                send(
                    x_send.at[stage, way],
                    x_halo.at[stage, way],
                    sem_x.at[0, stage, way],
                    sem_x.at[1, stage, way],
                    beside[way],
                )
            )
        for way in range(2):
            group = (up_g, dn_g)[way]
            for n, (start, size, brick) in enumerate(((0, 3, me_b), (3, 1, up_b), (4, 1, dn_b))):
                copies.append(
                    send(
                        row_send.at[stage, way, pl.ds(start, size)],
                        row_halo.at[stage, way, pl.ds(start, size)],
                        sem_row.at[0, stage, way, n],
                        sem_row.at[1, stage, way, n],
                        (group, brick),
                    )
                )
        return copies

    def stream(stage):
        moved = []
        for q in range(Q):
            cx, cy, cz = VELOCITY_SET[q]
            if cx == 0:
                value = post[stage, q]
            else:
                way = 0 if cx > 0 else 1
                value = x_halo[stage, way, TO_BRICK[way].index(q)]
            if cy:
                way = 0 if cy > 0 else 1
                edge = row_halo[stage, way, TO_GROUP[way].index(q)]
                value = pltpu.roll(value, 1 if cy > 0 else LY - 1, 0)
                value = jnp.where(first_row if cy > 0 else last_row, edge, value)
            if cz:
                value = pltpu.roll(value, 1 if cz > 0 else NZ - 1, 1)
            if cy:
                value = jnp.where(
                    low_wall if cy > 0 else high_wall, post[stage, OPPOSITE[q]], value
                )
            moved.append(value)
        return moved

    def kick_of(step, k, half):
        if step == 0:
            return cur[k, half.start // 8, 6]
        if k == 0:
            return kick_in[step, half]
        return halo_kick[k, step - 1, half]

    HALVES = (slice(0, 8), slice(8, 16))

    def load(step, k):
        for c, half in enumerate(HALVES):
            if k in (1, 3) and step:
                for axis in range(3):
                    speed = halo_vel[step - 1, k // 2, c, axis]
                    cur[k, c, 3 + axis] = speed
                    cur[k, c, axis] += TIME_STEP * speed
            tail = cur[k, c, 7]
            push = KICK_SCALE * kick_of(step, k, half)
            fields = [cur[k, c, axis] for axis in range(3)]
            fields += [FRICTION * cur[k, c, 3 + axis] for axis in range(3)]
            fields += [
                push + (REPEL_SAME + (REPEL_CROSS - REPEL_SAME) * tail),
                push + (REPEL_CROSS + (REPEL_SAME - REPEL_CROSS) * tail),
            ]
            for n, b in enumerate((-1, 0, 1)):
                for f, field in enumerate(fields):
                    if b:
                        field = pltpu.roll(field, (-b) % NZ, 1)
                    if f == 2:
                        field = field + float(b)
                    near[k, n, c, f] = field

    PLACE = (0, 1, -1, -2)

    def act(step, k, on, totals):
        sides = [(t, c) for t in on for c in range(2)]
        held = []
        for t, c in sides:
            apart = float(PLACE[k] - PLACE[t])
            x = cur[t, c, 0]
            held.append(
                (
                    x - apart * side if apart else x,
                    cur[t, c, 1],
                    cur[t, c, 2],
                    FRICTION * cur[t, c, 3],
                    FRICTION * cur[t, c, 4],
                    FRICTION * cur[t, c, 5],
                    KICK_SCALE * kick_of(step, t, HALVES[c]),
                    cur[t, c, 7] > 0.5,
                )
            )

        def tile(n, forces):
            forces = list(forces)
            for j in range(CAP):
                xj, yj, zj, uj, vj, wj, a0, a1 = [
                    near[k, n, j // 8, f, j % 8 : j % 8 + 1, :] for f in range(8)
                ]
                for i, (x, y, z, u, v, w, push, tail) in enumerate(held):
                    dx = x - xj
                    dy = y - yj
                    dz = z - zj
                    weight = jnp.maximum(1.0 - (dx * dx + dy * dy + dz * dz), 0.0)
                    closing = dx * (u - uj) + dy * (v - vj) + dz * (w - wj)
                    strength = weight * ((jnp.where(tail, a1, a0) + push) - weight * closing)
                    fx, fy, fz = forces[i]
                    forces[i] = (fx + strength * dx, fy + strength * dy, fz + strength * dz)
            return tuple(forces)

        forces = tuple(totals[side_] for side_ in sides)
        for n in range(3):
            forces = tile(n, forces)
        for side_, force in zip(sides, forces):
            totals[side_] = force

    def bond(t, totals):
        for c, half in enumerate(HALVES):
            places = [cur[t, c, axis] for axis in range(3)]
            found = list(places)
            for j in range(CAP):
                match = partners[t, half] == j
                for axis in range(3):
                    found[axis] = jnp.where(
                        match, cur[t, j // 8, axis, j % 8 : j % 8 + 1, :], found[axis]
                    )
            totals[t, c] = tuple(-BOND_STIFF * (p - f) for p, f in zip(places, found))

    def advance(step, t, totals, flow):
        for c in range(2):
            here = cur[t, c, 0] < 0.5 * FAR
            for axis in range(3):
                speed = cur[t, c, 3 + axis]
                force = totals[t, c][axis] + (flow[axis : axis + 1] - DRAG_RATE * speed)
                speed = jnp.where(here, speed + TIME_STEP * force, 0.0)
                cur[t, c, 3 + axis] = speed
                if t == 0 and step < STEPS - 1:
                    vel_send[step, c, axis] = speed
                if t == 0 and step == STEPS - 1:
                    vel_out[axis, HALVES[c]] = speed
            if step < STEPS - 1:
                for axis in range(3):
                    cur[t, c, axis] += TIME_STEP * cur[t, c, 3 + axis]

    def cell_copies():
        other = MIDDLE + 1 - mid
        targets = [(other, me_b, 0), (me_g, up_b, 2), (other, up_b, 2)]
        targets += [(me_g, dn_b, 1), (other, dn_b, 1)]
        copies = []
        for n, (group, brick, column) in enumerate(targets):
            copies.append(
                remote(
                    cells.at[0, mid],
                    cells.at[column, mid],
                    sem_cell.at[n],
                    sem_cell.at[5 + 2 * column + mid],
                    (group, brick),
                )
            )
        return copies

    def lattice_between():
        for copy in post_copies:
            copy.wait_recv()
        g = stream(0)
        density, inverse, velocity = moments(g)
        store_post(1, collide(g, density, inverse, velocity))
        copies = send_post(1)

        @pl.when(is_mid)
        def _():
            for n, value in enumerate([density] + velocity + [row_ids.astype(F32)]):
                cells[0, mid, n : n + 1, :] = jnp.sum(
                    jnp.where(at_cell, value, 0.0), axis=0, keepdims=True
                )
            for copy in cell_copies():
                copy.start()

        return copies

    def wait_drag(column):
        for n in range(2):

            def wait():
                remote(
                    drag.at[column, n],
                    drag.at[column, n],
                    sem_drag.at[0],
                    sem_drag.at[31 + 2 * column + n],
                    peers[0],
                ).wait_recv()

            if column:
                wait()
            else:
                pl.when(me_g != MIDDLE + n)(wait)
        return (DRAG_RATE / VELOCITY_SCALE) * (drag[column, 0, 0:3] + drag[column, 1, 0:3])

    totals = {}
    bond(0, totals)
    load(0, 0)
    act(0, 0, (0,), totals)
    cur_copies[1].wait_recv()
    load(0, 1)
    act(0, 1, (0,), totals)
    pl.semaphore_wait(sem_corner, 2)
    post_copies = send_post(0)
    cur_copies[2].wait_recv()
    partner_copies[2].wait_recv()
    bond(2, totals)
    load(0, 2)
    act(0, 2, (0, 2), totals)
    flow = wait_drag(0)
    for copy in cur_copies.values():
        copy.wait_send()
    advance(0, 0, totals, flow)
    vel_copies = {
        3: send(vel_send.at[0], halo_vel.at[0, 1], sem_vel.at[0, 2], sem_vel.at[1, 2], ahead2),
        1: send(vel_send.at[0], halo_vel.at[0, 0], sem_vel.at[0, 0], sem_vel.at[1, 0], pair[0]),
    }
    act(0, 0, (2,), totals)
    cur_copies[3].wait_recv()
    load(0, 3)
    act(0, 3, (2,), totals)

    later = {}
    for copy in kick_copies.values():
        copy.wait_recv()
    bond(0, later)
    load(1, 0)
    act(1, 0, (0,), later)
    vel_copies[1].wait_recv()
    load(1, 1)
    act(1, 1, (0,), later)
    post_copies = lattice_between()

    far_flow = wait_drag(1)
    advance(0, 2, totals, far_flow)
    totals = later
    bond(2, totals)
    load(1, 2)
    act(1, 2, (0, 2), totals)
    advance(1, 0, totals, flow)
    vel_copies[1] = send(
        vel_send.at[1], halo_vel.at[1, 0], sem_vel.at[0, 1], sem_vel.at[1, 1], pair[0]
    )
    act(1, 0, (2,), totals)
    vel_copies[3].wait_recv()
    load(1, 3)
    act(1, 3, (2,), totals)
    advance(1, 2, totals, far_flow)

    bond(0, totals)
    load(2, 0)
    act(2, 0, (0,), totals)
    load(2, 2)
    act(2, 2, (0,), totals)
    vel_copies[1].wait_recv()
    load(2, 1)
    act(2, 1, (0,), totals)
    advance(2, 0, totals, flow)

    for axis in range(3):
        sums[me_g, axis : axis + 1, :] = jnp.sum(
            cur[0, 0, 3 + axis] + cur[0, 1, 3 + axis], axis=0, keepdims=True
        )
    sums[me_g, 3:4, :] = count.astype(F32)
    for k in FARTHEST:
        remote(sums.at[me_g], sums.at[me_g], sem_sum.at[0], sem_sum.at[1], peers[k - 1]).start()
    for n in range(2):
        remote(
            sums.at[me_g], sums.at[GROUPS + me_g], sem_sum.at[0], sem_sum.at[2], far_mids[n]
        ).start()

    def all_sums(start, size, recv_sem):
        part = sums.at[pl.ds(start, size)]
        return remote(part, part, sem_sum.at[0], recv_sem, peers[0])

    for axis in range(3):
        for own, half in enumerate(HALVES):
            place = cur[0, own, axis] + TIME_STEP * cur[0, own, 3 + axis]
            pos_out[axis, half] = jnp.where(occupied[half], place, 0.0)
    for copy in post_copies:
        copy.wait_recv()
    g = stream(1)
    for q in range(Q):
        pop_out[q] = g[q]

    for copy in unsent:
        if not any(copy is other for other in cur_copies.values()):
            copy.wait_send()

    def pooled(which):
        total = sums[GROUPS * which]
        for n in range(1, GROUPS):
            total = total + sums[GROUPS * which + n]
        return total[0:3] / total[3:4]

    all_sums(0, GROUPS - 1, sem_sum.at[1]).wait_recv()
    mean = pooled(0)
    for axis in range(3):
        mean_out[axis] = mean[axis : axis + 1]

    @pl.when(is_mid)
    def _():
        means[2, 0:3] = mean
        mean_copy = remote(means.at[2], means.at[0], sem_mean.at[0], sem_mean.at[1], pair[0])
        mean_copy.start()
        for column in range(3):
            for n in range(2):
                wait = remote(
                    cells.at[0, mid],
                    cells.at[column, n],
                    sem_cell.at[0],
                    sem_cell.at[5 + 2 * column + n],
                    beside[0],
                )
                if column:
                    wait.wait_recv()
                else:

                    @pl.when(mid != n)
                    def _():
                        wait.wait_recv()

        def change(column, column_mean, members):
            cell = cells[column, 0] + cells[column, 1]
            density = cell[0:1]
            inverse = 1.0 / density
            row = cell[4:5].astype(jnp.int32)
            before, after = [], []
            for axis in range(3):
                speed = cell[1 + axis : 2 + axis]
                force = VELOCITY_SCALE * column_mean[axis : axis + 1] - speed
                pushed = speed + (RELAX_TIME * PUSH) * inverse if axis == 0 else speed
                before.append(pushed)
                after.append(pushed + RELAX_TIME * force * inverse)
            square = sum(a * a - b * b for a, b in zip(after, before))
            for q in members:
                cx, cy, cz = VELOCITY_SET[q]
                change = -1.5 * square
                if q:
                    a, b = along(q, after), along(q, before)
                    change = change + (a - b) * (3.0 + 4.5 * (a + b))
                change = (1.0 / RELAX_TIME) * density * change
                tile = jnp.where(row_ids == row + cy, change, 0.0)
                if cz:
                    tile = pltpu.roll(tile, 1 if cz > 0 else NZ - 1, 1)
                pop_out[q] += tile

        change(0, mean, [q for q in range(Q) if VELOCITY_SET[q][0] == 0])
        mean_copy.wait_recv()
        all_sums(GROUPS, GROUPS, sem_sum.at[2]).wait_recv()
        far_mean = pooled(1)
        near_mean = means[0, 0:3]
        change(1, jnp.where(even, near_mean, far_mean), TO_BRICK[1])
        change(2, jnp.where(even, far_mean, near_mean), TO_BRICK[0])
        mean_copy.wait_send()
        for copy in cell_copies():
            copy.wait_send()
        for copy in drag_copies():
            copy.wait_send()

    all_sums(0, GROUPS + 1, sem_sum.at[1]).wait_send()


def hand_out(*refs):
    sources, targets, sem = refs[:4], refs[4:8], refs[8]
    copies = [
        pltpu.make_async_copy(source, target, sem.at[n])
        for n, (source, target) in enumerate(zip(sources, targets))
    ]
    for copy in copies:
        copy.start()
    for copy in copies:
        copy.wait()


def local(
    populations, membrane_rows, positions, velocities, kicks, bead_types, bond_partner, tile_counts
):
    vmem = pl.BlockSpec(memory_space=pltpu.VMEM)
    hbm = pl.BlockSpec(memory_space=pltpu.HBM)
    anywhere = pl.BlockSpec(memory_space=pl.ANY)
    dma = pltpu.SemaphoreType.DMA
    bead = (CAP, NZ)
    outs = pl.pallas_call(
        kernel,
        out_shape=(
            pltpu.VMEM((Q, LY, NZ), F32),
            pltpu.VMEM((3, 1, NZ), F32),
            pltpu.VMEM((3, *bead), F32),
            pltpu.VMEM((3, *bead), F32),
        ),
        in_specs=[hbm] * 8,
        out_specs=[vmem] * 4,
        scratch_shapes=[
            pltpu.VMEM((Q, LY, NZ), F32),
            pltpu.VMEM((1, NZ), jnp.int32),
            pltpu.VMEM((3, *bead), F32),
            pltpu.VMEM((3, *bead), F32),
            pltpu.VMEM((STEPS, *bead), F32),
            pltpu.VMEM(bead, jnp.int32),
            pltpu.VMEM(bead, jnp.int32),
            pltpu.VMEM((1, NZ), jnp.int32),
            dma((8,)),
            pltpu.VMEM((4, 2, 8, 8, NZ), F32),
            pltpu.VMEM((3, *bead), jnp.int32),
            pltpu.VMEM((4, 2, *bead), F32),
            pltpu.VMEM((2, 2, 3, 8, NZ), F32),
            pltpu.VMEM((2, 2, 2, 3, 8, NZ), F32),
            pltpu.VMEM((4, 3, 2, 8, 8, NZ), F32),
            pltpu.VMEM((2, 2, 4, NZ), F32),
            pltpu.VMEM((2, Q, LY, NZ), F32),
            pltpu.VMEM((2, 2, 5, LY, NZ), F32),
            pltpu.VMEM((2, 2, 5, LY, NZ), F32),
            pltpu.VMEM((2, 2, 5, 1, NZ), F32),
            pltpu.VMEM((2, 2, 5, 1, NZ), F32),
            pltpu.VMEM((3, 2, 8, NZ), F32),
            pltpu.VMEM((2 * GROUPS, 4, NZ), F32),
            pltpu.VMEM((3, 8, NZ), F32),
            dma((2, 3)),
            dma((2, 3)),
            dma((2, 3)),
            dma((2, 3)),
            dma((35,)),
            dma((2, 2, 2)),
            dma((2, 2, 2, 3)),
            dma((11,)),
            dma((3,)),
            dma((2,)),
            pltpu.SemaphoreType.REGULAR,
        ],
        compiler_params=pltpu.CompilerParams(
            collective_id=0, has_side_effects=True, vmem_limit_bytes=4 << 20
        ),
        name="cycle",
    )(
        *(
            pltpu.with_memory_space_constraint(x, pltpu.HBM)
            for x in (
                populations.reshape(Q, LY, NZ),
                membrane_rows,
                positions.reshape(3, *bead),
                velocities.reshape(3, *bead),
                kicks.reshape(STEPS, *bead),
                bead_types.reshape(bead),
                bond_partner.reshape(bead),
                tile_counts.reshape(1, NZ),
            )
        )
    )
    second, mean, places, speeds = pl.pallas_call(
        hand_out,
        out_shape=tuple(jax.ShapeDtypeStruct(x.shape, F32) for x in outs),
        in_specs=[anywhere] * 4,
        out_specs=[hbm] * 4,
        scratch_shapes=[dma((4,))],
        compiler_params=pltpu.CompilerParams(vmem_limit_bytes=1 << 20),
        name="hand_out",
    )(*outs)
    return (
        second.reshape(Q, 1, LY, NZ),
        mean,
        places.reshape(1, 3, CAP, 1, NZ),
        speeds.reshape(1, 3, CAP, 1, NZ),
    )


def solution(mesh):
    return jax.shard_map(
        local,
        mesh=mesh,
        in_specs=(
            P(None, "brick", "group", None),
            P("brick", None),
            P("group", None, None, "brick", None),
            P("group", None, None, "brick", None),
            P("group", None, None, "brick", None),
            P("group", None, "brick", None),
            P("group", None, "brick", None),
            P("group", "brick", None),
        ),
        out_specs=(
            P(None, "brick", "group", None),
            P(None, "brick", None),
            P("group", None, None, "brick", None),
            P("group", None, None, "brick", None),
        ),
        check_vma=False,
    )
```

```python
import math

import jax
import jax.numpy as jnp
import numpy as np
from jax import lax
from jax.experimental import pallas as pl
from jax.experimental.pallas import tpu as pltpu
from jax.sharding import PartitionSpec as P

VELOCITY_SET = (
    (0, 0, 0),
    (1, 0, 0),
    (-1, 0, 0),
    (0, 1, 0),
    (0, -1, 0),
    (0, 0, 1),
    (0, 0, -1),
    (1, 1, 0),
    (-1, -1, 0),
    (1, -1, 0),
    (-1, 1, 0),
    (1, 0, 1),
    (-1, 0, -1),
    (1, 0, -1),
    (-1, 0, 1),
    (0, 1, 1),
    (0, -1, -1),
    (0, 1, -1),
    (0, -1, 1),
)
WEIGHT_SET = (1.0 / 3.0,) + (1.0 / 18.0,) * 6 + (1.0 / 36.0,) * 12
OPPOSITE = (0, 2, 1, 4, 3, 6, 5, 8, 7, 10, 9, 12, 11, 14, 13, 16, 15, 18, 17)
Q = 19
TO_BRICK = ((1, 7, 9, 11, 13), (2, 8, 10, 12, 14))
TO_GROUP = ((3, 15, 17, 7, 10), (4, 16, 18, 9, 8))
RELAX_TIME = 0.8
PUSH = 0.001
VELOCITY_SCALE = 0.1
DRAG_RATE = 5.0
REPEL_SAME = 25.0
REPEL_CROSS = 50.0
FRICTION = 4.5
KICK_SCALE = 3.0 / math.sqrt(0.02) / math.sqrt(2.0)
TIME_STEP = 0.02
BOND_STIFF = 10.0
FAR = 1.0e8

GROUPS, BRICKS = 16, 32
CAP, NZ, LY, STEPS = 16, 128, 8, 3
MIDDLE = 7
FARTHEST = (8, 7, 9, 6, 10, 5, 11, 4, 12, 3, 13, 2, 14, 1, 15)
MESH = pl.DeviceIdType.MESH
F32 = jnp.float32


def moments(g):
    def total(signs):
        parts = []
        for weight, members in ((1.0 / 18.0, range(1, 7)), (1.0 / 36.0, range(7, 19))):
            part = None
            for q in members:
                if signs[q]:
                    if part is None:
                        part = g[q] if signs[q] > 0 else -g[q]
                    else:
                        part = part + g[q] if signs[q] > 0 else part - g[q]
            parts.append(part * weight)
        return parts[0] + parts[1]

    density = g[0] * (1.0 / 3.0) + total((1,) * Q)
    inverse = 1.0 / density
    velocity = [total([c[axis] for c in VELOCITY_SET]) * inverse for axis in range(3)]
    return density, inverse, velocity


def along(q, s):
    value = None
    for axis in range(3):
        sign = VELOCITY_SET[q][axis]
        if sign:
            if value is None:
                value = s[axis] if sign > 0 else -s[axis]
            else:
                value = value + s[axis] if sign > 0 else value - s[axis]
    return value


def collide(g, density, inverse, velocity):
    s = [velocity[0] + (RELAX_TIME * PUSH) * inverse, velocity[1], velocity[2]]
    rest = 1.0 - 1.5 * (s[0] * s[0] + s[1] * s[1] + s[2] * s[2])
    post = []
    for q in range(Q):
        if q == 0:
            equilibrium = density * rest
        else:
            a = along(q, s)
            equilibrium = density * (rest + a * (3.0 + 4.5 * a))
        post.append(g[q] - (g[q] - equilibrium) * (1.0 / RELAX_TIME))
    return post


def kernel(
    pop_hbm,
    rows_hbm,
    pos_hbm,
    vel_hbm,
    kick_hbm,
    type_hbm,
    partner_hbm,
    count_hbm,
    pop_out,
    mean_out,
    pos_out,
    vel_out,
    pop_in,
    rows_in,
    pos_in,
    vel_in,
    kick_in,
    type_in,
    partner_in,
    count_in,
    sem_in,
    cur,
    partners,
    halo_kick,
    vel_send,
    halo_vel,
    near,
    drag,
    post,
    x_send,
    x_halo,
    row_send,
    row_halo,
    cells,
    sums,
    means,
    sem_cur,
    sem_partner,
    sem_kick,
    sem_vel,
    sem_drag,
    sem_x,
    sem_row,
    sem_cell,
    sem_sum,
    sem_mean,
    sem_corner,
):
    me_g = lax.axis_index("group")
    me_b = lax.axis_index("brick")
    up_b = lax.rem(me_b + 1, BRICKS)
    dn_b = lax.rem(me_b + BRICKS - 1, BRICKS)
    up_g = lax.rem(me_g + 1, GROUPS)
    dn_g = lax.rem(me_g + GROUPS - 1, GROUPS)
    is_mid = (me_g == MIDDLE) | (me_g == MIDDLE + 1)
    mid = jnp.where(me_g == MIDDLE, 0, 1)
    peers = [(lax.rem(me_g + k, GROUPS), me_b) for k in range(1, GROUPS)]
    beside = [(me_g, up_b), (me_g, dn_b)]
    even = lax.rem(me_b, 2) == 0
    pair = [(me_g, jnp.where(even, up_b, dn_b)), (me_g, jnp.where(even, dn_b, up_b))]
    side = jnp.where(even, 1.0, -1.0)
    ahead2 = (me_g, lax.rem(me_b + jnp.where(even, 2, BRICKS - 2), BRICKS))
    back2 = (me_g, lax.rem(me_b + jnp.where(even, BRICKS - 2, 2), BRICKS))
    targets = [pair[0], pair[1], ahead2]

    far_mids = [(MIDDLE, pair[1][1]), (MIDDLE + 1, pair[1][1])]

    barrier = pltpu.get_barrier_semaphore()
    pl.semaphore_signal(barrier, inc=1, device_id=pair[1], device_id_type=MESH)

    loads = {}
    for n, (name, source, target) in enumerate(
        (
            ("pos", pos_hbm, pos_in),
            ("vel", vel_hbm, vel_in),
            ("kick", kick_hbm, kick_in),
            ("type", type_hbm, type_in),
            ("count", count_hbm, count_in),
            ("pop", pop_hbm, pop_in),
            ("rows", rows_hbm, rows_in),
            ("partner", partner_hbm, partner_in),
        )
    ):
        loads[name] = pltpu.make_async_copy(source, target, sem_in.at[n])
        loads[name].start()

    for device in (pair[0], back2):
        pl.semaphore_signal(barrier, inc=1, device_id=device, device_id_type=MESH)
    for n in range(2):
        pl.semaphore_signal(barrier, inc=1, device_id=far_mids[n], device_id_type=MESH)

        @pl.when(me_g != MIDDLE + n)
        def _():
            pl.semaphore_signal(
                barrier, inc=1, device_id=(MIDDLE + n, me_b), device_id_type=MESH
            )

    for group in (up_g, dn_g):
        pl.semaphore_signal(barrier, inc=1, device_id=(group, me_b), device_id_type=MESH)

    unsent = []

    def remote(src, dst, send_sem, recv_sem, device):
        return pltpu.make_async_remote_copy(
            src_ref=src,
            dst_ref=dst,
            send_sem=send_sem,
            recv_sem=recv_sem,
            device_id=device,
            device_id_type=MESH,
        )

    def send(*args):
        copy = remote(*args)
        copy.start()
        unsent.append(copy)
        return copy

    for name in ("pos", "vel", "kick", "type", "count", "partner"):
        loads[name].wait()
    slot_ids = lax.broadcasted_iota(jnp.int32, (CAP, NZ), 0)
    count = count_in[...]
    occupied = slot_ids < count
    tails = type_in[...].astype(F32)
    partner = partner_in[...]
    partners[0] = jnp.where(partner < count, partner, slot_ids)
    for c in range(2):
        half = slice(8 * c, 8 * c + 8)
        cur[0, c, 0] = jnp.where(occupied[half], pos_in[0, half], FAR)
        for axis in range(1, 3):
            cur[0, c, axis] = pos_in[axis, half]
        for axis in range(3):
            cur[0, c, 3 + axis] = vel_in[axis, half]
        cur[0, c, 6] = kick_in[0, half]
        cur[0, c, 7] = tails[half]

    pl.semaphore_wait(barrier, jnp.where(is_mid, 5 + 2 * GROUPS - 1, 5))

    def spread(source, target, sems, which):
        return {
            k: send(source, target.at[k], sems.at[0, k - 1], sems.at[1, k - 1], targets[k - 1])
            for k in which
        }

    cur_copies = spread(cur.at[0], cur, sem_cur, (2, 1))
    partner_copies = spread(partners.at[0], partners, sem_partner, (2,))

    for group in (up_g, dn_g):
        pl.semaphore_signal(sem_corner, inc=1, device_id=(group, me_b), device_id_type=MESH)

    row_ids = me_g * LY + lax.broadcasted_iota(jnp.int32, (LY, NZ), 0)
    first_row = lax.broadcasted_iota(jnp.int32, (LY, NZ), 0) == 0
    last_row = lax.broadcasted_iota(jnp.int32, (LY, NZ), 0) == LY - 1
    low_wall = first_row & (me_g == 0)
    high_wall = last_row & (me_g == GROUPS - 1)

    for name in ("pop", "rows"):
        loads[name].wait()
    at_cell = row_ids == rows_in[...]
    g = [pop_in[q] for q in range(Q)]
    density, inverse, velocity = moments(g)

    def drag_copies():
        copies = [
            remote(drag.at[0, mid], drag.at[0, mid], sem_drag.at[15 + k], sem_drag.at[31 + mid], peers[k - 1])
            for k in FARTHEST
        ]
        return copies + [
            remote(drag.at[0, mid], drag.at[1, mid], sem_drag.at[n], sem_drag.at[33 + mid], (n, pair[1][1]))
            for n in range(GROUPS)
        ]

    @pl.when(is_mid)
    def _():
        for axis in range(3):
            drag[0, mid, axis : axis + 1, :] = jnp.sum(
                jnp.where(at_cell, velocity[axis], 0.0), axis=0, keepdims=True
            )
        for copy in drag_copies():
            copy.start()

    def store_post(stage, values):
        for q in range(Q):
            post[stage, q] = values[q]
        for way in range(2):
            for n, q in enumerate(TO_BRICK[way]):
                x_send[stage, way, n] = values[q]
            edge = LY - 1 if way == 0 else 0
            for n, q in enumerate(TO_GROUP[way]):
                row_send[stage, way, n] = values[q][edge : edge + 1, :]

    store_post(0, collide(g, density, inverse, velocity))

    cur_copies.update(spread(cur.at[0], cur, sem_cur, (3,)))
    kick_copies = spread(kick_in.at[pl.ds(1, 2)], halo_kick, sem_kick, (2, 1))
    kick_copies[3] = send(
        kick_in.at[1], halo_kick.at[3, 0], sem_kick.at[0, 2], sem_kick.at[1, 2], ahead2
    )

    def send_post(stage):
        copies = []
        for way in range(2):
            copies.append(
                send(
                    x_send.at[stage, way],
                    x_halo.at[stage, way],
                    sem_x.at[0, stage, way],
                    sem_x.at[1, stage, way],
                    beside[way],
                )
            )
        for way in range(2):
            group = (up_g, dn_g)[way]
            for n, (start, size, brick) in enumerate(((0, 3, me_b), (3, 1, up_b), (4, 1, dn_b))):
                copies.append(
                    send(
                        row_send.at[stage, way, pl.ds(start, size)],
                        row_halo.at[stage, way, pl.ds(start, size)],
                        sem_row.at[0, stage, way, n],
                        sem_row.at[1, stage, way, n],
                        (group, brick),
                    )
                )
        return copies

    def stream(stage):
        moved = []
        for q in range(Q):
            cx, cy, cz = VELOCITY_SET[q]
            if cx == 0:
                value = post[stage, q]
            else:
                way = 0 if cx > 0 else 1
                value = x_halo[stage, way, TO_BRICK[way].index(q)]
            if cy:
                way = 0 if cy > 0 else 1
                edge = row_halo[stage, way, TO_GROUP[way].index(q)]
                value = pltpu.roll(value, 1 if cy > 0 else LY - 1, 0)
                value = jnp.where(first_row if cy > 0 else last_row, edge, value)
            if cz:
                value = pltpu.roll(value, 1 if cz > 0 else NZ - 1, 1)
            if cy:
                value = jnp.where(
                    low_wall if cy > 0 else high_wall, post[stage, OPPOSITE[q]], value
                )
            moved.append(value)
        return moved

    def kick_of(step, k, half):
        if step == 0:
            return cur[k, half.start // 8, 6]
        if k == 0:
            return kick_in[step, half]
        return halo_kick[k, step - 1, half]

    HALVES = (slice(0, 8), slice(8, 16))

    def load(step, k):
        for c, half in enumerate(HALVES):
            if k in (1, 3) and step:
                for axis in range(3):
                    speed = halo_vel[step - 1, k // 2, c, axis]
                    cur[k, c, 3 + axis] = speed
                    cur[k, c, axis] += TIME_STEP * speed
            tail = cur[k, c, 7]
            push = KICK_SCALE * kick_of(step, k, half)
            fields = [cur[k, c, axis] for axis in range(3)]
            fields += [FRICTION * cur[k, c, 3 + axis] for axis in range(3)]
            fields += [
                push + (REPEL_SAME + (REPEL_CROSS - REPEL_SAME) * tail),
                push + (REPEL_CROSS + (REPEL_SAME - REPEL_CROSS) * tail),
            ]
            for n, b in enumerate((-1, 0, 1)):
                for f, field in enumerate(fields):
                    if b:
                        field = pltpu.roll(field, (-b) % NZ, 1)
                    if f == 2:
                        field = field + float(b)
                    near[k, n, c, f] = field

    PLACE = (0, 1, -1, -2)

    def act(step, k, on, totals):
        sides = [(t, c) for t in on for c in range(2)]
        held = []
        for t, c in sides:
            apart = float(PLACE[k] - PLACE[t])
            x = cur[t, c, 0]
            held.append(
                (
                    x - apart * side if apart else x,
                    cur[t, c, 1],
                    cur[t, c, 2],
                    FRICTION * cur[t, c, 3],
                    FRICTION * cur[t, c, 4],
                    FRICTION * cur[t, c, 5],
                    KICK_SCALE * kick_of(step, t, HALVES[c]),
                    cur[t, c, 7] > 0.5,
                )
            )

        def tile(n, forces):
            forces = list(forces)
            for j in range(CAP):
                xj, yj, zj, uj, vj, wj, a0, a1 = [
                    near[k, n, j // 8, f, j % 8 : j % 8 + 1, :] for f in range(8)
                ]
                for i, (x, y, z, u, v, w, push, tail) in enumerate(held):
                    dx = x - xj
                    dy = y - yj
                    dz = z - zj
                    weight = jnp.maximum(1.0 - (dx * dx + dy * dy + dz * dz), 0.0)
                    closing = dx * (u - uj) + dy * (v - vj) + dz * (w - wj)
                    strength = weight * ((jnp.where(tail, a1, a0) + push) - weight * closing)
                    fx, fy, fz = forces[i]
                    forces[i] = (fx + strength * dx, fy + strength * dy, fz + strength * dz)
            return tuple(forces)

        forces = tuple(totals[side_] for side_ in sides)
        for n in range(3):
            forces = tile(n, forces)
        for side_, force in zip(sides, forces):
            totals[side_] = force

    def bond(t, totals):
        for c, half in enumerate(HALVES):
            places = [cur[t, c, axis] for axis in range(3)]
            found = list(places)
            for j in range(CAP):
                match = partners[t, half] == j
                for axis in range(3):
                    found[axis] = jnp.where(
                        match, cur[t, j // 8, axis, j % 8 : j % 8 + 1, :], found[axis]
                    )
            totals[t, c] = tuple(-BOND_STIFF * (p - f) for p, f in zip(places, found))

    def advance(step, t, totals, flow):
        for c in range(2):
            here = cur[t, c, 0] < 0.5 * FAR
            for axis in range(3):
                speed = cur[t, c, 3 + axis]
                force = totals[t, c][axis] + (flow[axis : axis + 1] - DRAG_RATE * speed)
                speed = jnp.where(here, speed + TIME_STEP * force, 0.0)
                cur[t, c, 3 + axis] = speed
                if t == 0 and step < STEPS - 1:
                    vel_send[step, c, axis] = speed
                if t == 0 and step == STEPS - 1:
                    vel_out[axis, HALVES[c]] = speed
            if step < STEPS - 1:
                for axis in range(3):
                    cur[t, c, axis] += TIME_STEP * cur[t, c, 3 + axis]

    def cell_copies():
        other = MIDDLE + 1 - mid
        targets = [(other, me_b, 0), (me_g, up_b, 2), (other, up_b, 2)]
        targets += [(me_g, dn_b, 1), (other, dn_b, 1)]
        copies = []
        for n, (group, brick, column) in enumerate(targets):
            copies.append(
                remote(
                    cells.at[0, mid],
                    cells.at[column, mid],
                    sem_cell.at[n],
                    sem_cell.at[5 + 2 * column + mid],
                    (group, brick),
                )
            )
        return copies

    def lattice_between():
        for copy in post_copies:
            copy.wait_recv()
        g = stream(0)
        density, inverse, velocity = moments(g)
        store_post(1, collide(g, density, inverse, velocity))
        copies = send_post(1)

        @pl.when(is_mid)
        def _():
            for n, value in enumerate([density] + velocity + [row_ids.astype(F32)]):
                cells[0, mid, n : n + 1, :] = jnp.sum(
                    jnp.where(at_cell, value, 0.0), axis=0, keepdims=True
                )
            for copy in cell_copies():
                copy.start()

        return copies

    def wait_drag(column):
        for n in range(2):

            def wait():
                remote(
                    drag.at[column, n],
                    drag.at[column, n],
                    sem_drag.at[0],
                    sem_drag.at[31 + 2 * column + n],
                    peers[0],
                ).wait_recv()

            if column:
                wait()
            else:
                pl.when(me_g != MIDDLE + n)(wait)
        return (DRAG_RATE / VELOCITY_SCALE) * (drag[column, 0, 0:3] + drag[column, 1, 0:3])

    totals = {}
    bond(0, totals)
    load(0, 0)
    act(0, 0, (0,), totals)
    cur_copies[1].wait_recv()
    load(0, 1)
    act(0, 1, (0,), totals)
    pl.semaphore_wait(sem_corner, 2)
    post_copies = send_post(0)
    cur_copies[2].wait_recv()
    partner_copies[2].wait_recv()
    bond(2, totals)
    load(0, 2)
    act(0, 2, (0, 2), totals)
    flow = wait_drag(0)
    for copy in cur_copies.values():
        copy.wait_send()
    advance(0, 0, totals, flow)
    vel_copies = {
        3: send(vel_send.at[0], halo_vel.at[0, 1], sem_vel.at[0, 2], sem_vel.at[1, 2], ahead2),
        1: send(vel_send.at[0], halo_vel.at[0, 0], sem_vel.at[0, 0], sem_vel.at[1, 0], pair[0]),
    }
    act(0, 0, (2,), totals)
    cur_copies[3].wait_recv()
    load(0, 3)
    act(0, 3, (2,), totals)

    later = {}
    for copy in kick_copies.values():
        copy.wait_recv()
    bond(0, later)
    load(1, 0)
    act(1, 0, (0,), later)
    vel_copies[1].wait_recv()
    load(1, 1)
    act(1, 1, (0,), later)
    post_copies = lattice_between()

    far_flow = wait_drag(1)
    advance(0, 2, totals, far_flow)
    totals = later
    bond(2, totals)
    load(1, 2)
    act(1, 2, (0, 2), totals)
    advance(1, 0, totals, flow)
    vel_copies[1] = send(
        vel_send.at[1], halo_vel.at[1, 0], sem_vel.at[0, 1], sem_vel.at[1, 1], pair[0]
    )
    act(1, 0, (2,), totals)

    later = {}
    bond(0, later)
    load(2, 0)
    act(2, 0, (0,), later)
    def with_near(forces):
        found = {(0, c): forces[c] for c in range(2)}
        vel_copies[1].wait_recv()
        load(2, 1)
        act(2, 1, (0,), found)
        return found[0, 0], found[0, 1]

    def with_far(forces):
        found = {(0, c): forces[c] for c in range(2)}
        far_totals = {(2, c): totals[2, c] for c in range(2)}
        vel_copies[3].wait_recv()
        load(1, 3)
        act(1, 3, (2,), far_totals)
        advance(1, 2, far_totals, far_flow)
        load(2, 2)
        act(2, 2, (0,), found)
        return found[0, 0], found[0, 1]

    slow_far = lax.rem((me_b + 1) // 2, 2) == 0
    forces = lax.fori_loop(
        0,
        2,
        lambda turn, forces: lax.cond((turn == 0) == slow_far, with_near, with_far, forces),
        (later[0, 0], later[0, 1]),
    )
    later = {(0, c): forces[c] for c in range(2)}
    advance(2, 0, later, flow)

    for axis in range(3):
        sums[me_g, axis : axis + 1, :] = jnp.sum(
            cur[0, 0, 3 + axis] + cur[0, 1, 3 + axis], axis=0, keepdims=True
        )
    sums[me_g, 3:4, :] = count.astype(F32)
    for n in range(2):
        remote(
            sums.at[me_g], sums.at[GROUPS + me_g], sem_sum.at[0], sem_sum.at[2], far_mids[n]
        ).start()
    for k in FARTHEST:
        remote(sums.at[me_g], sums.at[me_g], sem_sum.at[0], sem_sum.at[1], peers[k - 1]).start()

    def all_sums(start, size, recv_sem):
        part = sums.at[pl.ds(start, size)]
        return remote(part, part, sem_sum.at[0], recv_sem, peers[0])

    for axis in range(3):
        for own, half in enumerate(HALVES):
            place = cur[0, own, axis] + TIME_STEP * cur[0, own, 3 + axis]
            pos_out[axis, half] = jnp.where(occupied[half], place, 0.0)
    for copy in post_copies:
        copy.wait_recv()
    g = stream(1)
    for q in range(Q):
        pop_out[q] = g[q]

    for copy in unsent:
        if not any(copy is other for other in cur_copies.values()):
            copy.wait_send()

    def pooled(which):
        total = sums[GROUPS * which]
        for n in range(1, GROUPS):
            total = total + sums[GROUPS * which + n]
        return total[0:3] / total[3:4]

    all_sums(0, GROUPS - 1, sem_sum.at[1]).wait_recv()
    mean = pooled(0)
    for axis in range(3):
        mean_out[axis] = mean[axis : axis + 1]

    @pl.when(is_mid)
    def _():
        means[2, 0:3] = mean
        mean_copy = remote(means.at[2], means.at[0], sem_mean.at[0], sem_mean.at[1], pair[0])
        mean_copy.start()
        for column in range(3):
            for n in range(2):
                wait = remote(
                    cells.at[0, mid],
                    cells.at[column, n],
                    sem_cell.at[0],
                    sem_cell.at[5 + 2 * column + n],
                    beside[0],
                )
                if column:
                    wait.wait_recv()
                else:

                    @pl.when(mid != n)
                    def _():
                        wait.wait_recv()

        def change(column, column_mean, members):
            cell = cells[column, 0] + cells[column, 1]
            density = cell[0:1]
            inverse = 1.0 / density
            row = cell[4:5].astype(jnp.int32)
            before, after = [], []
            for axis in range(3):
                speed = cell[1 + axis : 2 + axis]
                force = VELOCITY_SCALE * column_mean[axis : axis + 1] - speed
                pushed = speed + (RELAX_TIME * PUSH) * inverse if axis == 0 else speed
                before.append(pushed)
                after.append(pushed + RELAX_TIME * force * inverse)
            square = sum(a * a - b * b for a, b in zip(after, before))
            for q in members:
                cx, cy, cz = VELOCITY_SET[q]
                change = -1.5 * square
                if q:
                    a, b = along(q, after), along(q, before)
                    change = change + (a - b) * (3.0 + 4.5 * (a + b))
                change = (1.0 / RELAX_TIME) * density * change
                tile = jnp.where(row_ids == row + cy, change, 0.0)
                if cz:
                    tile = pltpu.roll(tile, 1 if cz > 0 else NZ - 1, 1)
                pop_out[q] += tile

        change(0, mean, [q for q in range(Q) if VELOCITY_SET[q][0] == 0])
        mean_copy.wait_recv()
        all_sums(GROUPS, GROUPS, sem_sum.at[2]).wait_recv()
        far_mean = pooled(1)
        near_mean = means[0, 0:3]
        change(1, jnp.where(even, near_mean, far_mean), TO_BRICK[1])
        change(2, jnp.where(even, far_mean, near_mean), TO_BRICK[0])
        mean_copy.wait_send()
        for copy in cell_copies():
            copy.wait_send()
        for copy in drag_copies():
            copy.wait_send()

    all_sums(0, GROUPS + 1, sem_sum.at[1]).wait_send()


def hand_out(*refs):
    sources, targets, sem = refs[:4], refs[4:8], refs[8]
    copies = [
        pltpu.make_async_copy(source, target, sem.at[n])
        for n, (source, target) in enumerate(zip(sources, targets))
    ]
    for copy in copies:
        copy.start()
    for copy in copies:
        copy.wait()


def local(
    populations, membrane_rows, positions, velocities, kicks, bead_types, bond_partner, tile_counts
):
    vmem = pl.BlockSpec(memory_space=pltpu.VMEM)
    hbm = pl.BlockSpec(memory_space=pltpu.HBM)
    anywhere = pl.BlockSpec(memory_space=pl.ANY)
    dma = pltpu.SemaphoreType.DMA
    bead = (CAP, NZ)
    outs = pl.pallas_call(
        kernel,
        out_shape=(
            pltpu.VMEM((Q, LY, NZ), F32),
            pltpu.VMEM((3, 1, NZ), F32),
            pltpu.VMEM((3, *bead), F32),
            pltpu.VMEM((3, *bead), F32),
        ),
        in_specs=[hbm] * 8,
        out_specs=[vmem] * 4,
        scratch_shapes=[
            pltpu.VMEM((Q, LY, NZ), F32),
            pltpu.VMEM((1, NZ), jnp.int32),
            pltpu.VMEM((3, *bead), F32),
            pltpu.VMEM((3, *bead), F32),
            pltpu.VMEM((STEPS, *bead), F32),
            pltpu.VMEM(bead, jnp.int32),
            pltpu.VMEM(bead, jnp.int32),
            pltpu.VMEM((1, NZ), jnp.int32),
            dma((8,)),
            pltpu.VMEM((4, 2, 8, 8, NZ), F32),
            pltpu.VMEM((3, *bead), jnp.int32),
            pltpu.VMEM((4, 2, *bead), F32),
            pltpu.VMEM((2, 2, 3, 8, NZ), F32),
            pltpu.VMEM((2, 2, 2, 3, 8, NZ), F32),
            pltpu.VMEM((4, 3, 2, 8, 8, NZ), F32),
            pltpu.VMEM((2, 2, 4, NZ), F32),
            pltpu.VMEM((2, Q, LY, NZ), F32),
            pltpu.VMEM((2, 2, 5, LY, NZ), F32),
            pltpu.VMEM((2, 2, 5, LY, NZ), F32),
            pltpu.VMEM((2, 2, 5, 1, NZ), F32),
            pltpu.VMEM((2, 2, 5, 1, NZ), F32),
            pltpu.VMEM((3, 2, 8, NZ), F32),
            pltpu.VMEM((2 * GROUPS, 4, NZ), F32),
            pltpu.VMEM((3, 8, NZ), F32),
            dma((2, 3)),
            dma((2, 3)),
            dma((2, 3)),
            dma((2, 3)),
            dma((35,)),
            dma((2, 2, 2)),
            dma((2, 2, 2, 3)),
            dma((11,)),
            dma((3,)),
            dma((2,)),
            pltpu.SemaphoreType.REGULAR,
        ],
        compiler_params=pltpu.CompilerParams(
            collective_id=0, has_side_effects=True, vmem_limit_bytes=4 << 20
        ),
        name="cycle",
    )(
        *(
            pltpu.with_memory_space_constraint(x, pltpu.HBM)
            for x in (
                populations.reshape(Q, LY, NZ),
                membrane_rows,
                positions.reshape(3, *bead),
                velocities.reshape(3, *bead),
                kicks.reshape(STEPS, *bead),
                bead_types.reshape(bead),
                bond_partner.reshape(bead),
                tile_counts.reshape(1, NZ),
            )
        )
    )
    second, mean, places, speeds = pl.pallas_call(
        hand_out,
        out_shape=tuple(jax.ShapeDtypeStruct(x.shape, F32) for x in outs),
        in_specs=[anywhere] * 4,
        out_specs=[hbm] * 4,
        scratch_shapes=[dma((4,))],
        compiler_params=pltpu.CompilerParams(vmem_limit_bytes=1 << 20),
        name="hand_out",
    )(*outs)
    return (
        second.reshape(Q, 1, LY, NZ),
        mean,
        places.reshape(1, 3, CAP, 1, NZ),
        speeds.reshape(1, 3, CAP, 1, NZ),
    )


def solution(mesh):
    return jax.shard_map(
        local,
        mesh=mesh,
        in_specs=(
            P(None, "brick", "group", None),
            P("brick", None),
            P("group", None, None, "brick", None),
            P("group", None, None, "brick", None),
            P("group", None, None, "brick", None),
            P("group", None, "brick", None),
            P("group", None, "brick", None),
            P("group", "brick", None),
        ),
        out_specs=(
            P(None, "brick", "group", None),
            P(None, "brick", None),
            P("group", None, None, "brick", None),
            P("group", None, None, "brick", None),
        ),
        check_vma=False,
    )
```
